128 devices in a mesh: step: 16 (over z, x), seq: 8 (over y, core).
Axes of the slice: x: 4, y: 4, z: 4, core: 2. Of those that a mesh axis runs over, the one named last changes fastest.
Arguments:
- start_state: float32 [1024, 1536], P('seq'), may hold values from -6 to 6
- timesteps: int32 [32], P('step'), may hold values from 0 to 999, as said below
- qkv_weight: bfloat16 [1536, 6144], replicated
- out_weight: bfloat16 [2048, 1536], P('seq'), may hold values from -0.5 to 0.5
Outputs:
- trajectory: float32 [32, 1024, 1536], P('step', 'seq')
The draws below stay inside these ranges and needn't reach their ends.
Inputs may be any that keep to these rules, and one draw needn't show every extreme that they name: `timesteps`: distinct, falling along the steps, the first step at the maximum and the last at the minimum.
All inputs are finite; a program needn't handle non-finite values.
Results may differ from the reference program's by a relative error of at most 0.0029.
Values may be sent and summed in bfloat16 or wider, within the bound.
A program may use at most 128 MiB of HBM per device.

```python
import math
import jax
import jax.numpy as jnp
from jax import lax

D = 1536
HEADS = 16
HEAD_SIZE = 128
INNER = 2048
ITERS = 2
STEPS = 32
TOKENS = 1024


def draw_timesteps(key, part):
    key = jax.random.fold_in(key, 5)
    interior = jax.random.permutation(key, 998)[:STEPS - 2] + 1
    interior = -jnp.sort(-interior)
    first_value = jnp.full((1,), 999, jnp.int32)
    last_value = jnp.zeros((1,), jnp.int32)
    return jnp.concatenate([first_value, interior.astype(jnp.int32), last_value]).astype(jnp.int32)


def draw_qkv_weight(key, part):
    key = jax.random.fold_in(key, 11)
    key_query, key_keys, key_values = jax.random.split(key, 3)
    inner_width = HEADS * HEAD_SIZE
    query_part = 1.5 * jax.random.normal(key_query, (D, inner_width), jnp.float32)
    keys_part = 1.5 * jax.random.normal(key_keys, (D, inner_width), jnp.float32)
    values_part = jax.random.normal(key_values, (D, inner_width), jnp.float32)
    joined = jnp.concatenate([query_part, keys_part, values_part], axis=1) * D ** (-0.5)
    return joined.astype(jnp.bfloat16)


def block_levels(stream_key, dims, shards, low, top_value):
    loudness, own = 1.0, jax.random.fold_in(stream_key, 6)
    for dim, shards_of in shards:
        draws = jnp.exp(jax.random.uniform(jax.random.fold_in(own, dim), (shards_of,), jnp.float32, low / len(shards), top_value / len(shards)))
        loudness = loudness * jnp.repeat(draws, dims[dim] // shards_of).reshape([-1 if axis == dim else 1 for axis in range(len(dims))])
    return loudness


def gaussian(stream_key, dims, deviation, most, cuts=(), kind=jnp.bfloat16):
    values = deviation * jax.random.normal(stream_key, dims, jnp.float32)
    if cuts:
        values = values * block_levels(stream_key, dims, cuts, -0.22, 0.18)
    return jnp.clip(values, -most, most).astype(kind)


def setup_inputs(seed: int = 0) -> dict:
    seeds = jax.random.split(jax.random.key(seed), 5)
    start_state = gaussian(seeds[0], (TOKENS, D), 1.0, 6.0, ((0, 8),), jnp.float32)
    timesteps = draw_timesteps(jax.random.fold_in(seeds[4], 71), 0)
    qkv_weight = draw_qkv_weight(jax.random.fold_in(seeds[4], 71), 0)
    out_weight = gaussian(seeds[3], (INNER, D), HEAD_SIZE ** -0.5, 0.5, ((0, 8),))
    return dict(start_state=start_state, timesteps=timesteps, qkv_weight=qkv_weight, out_weight=out_weight)


norm_eps = 1e-06

def embed(step_index, model_width):
    half_width = model_width // 2
    frequency = jnp.exp(-math.log(10000.0) * jnp.arange(half_width, dtype=jnp.float32) / half_width)
    angles = step_index.astype(jnp.float32)[:, None] * frequency[None, :]
    return jnp.concatenate([jnp.sin(angles), jnp.cos(angles)], axis=1)

def one_head(pieces):
    query_rows, key_rows, value_rows = pieces
    scores = jnp.dot(query_rows, key_rows.T, preferred_element_type=jnp.float32) * (1.0 / math.sqrt(HEAD_SIZE))
    peak = lax.optimization_barrier(jnp.max(scores, axis=1, keepdims=True))
    expo = jnp.exp(scores - peak)
    softmax_total = lax.optimization_barrier(jnp.sum(expo, axis=1, keepdims=True))
    softmax_weights = (expo / softmax_total).astype(jnp.bfloat16)
    return jnp.dot(softmax_weights, value_rows, preferred_element_type=jnp.float32).astype(jnp.bfloat16)

def drift_of(state_row, embed_row, qkv_weight, out_weight):
    shifted = state_row + embed_row[None, :]
    mean_square = lax.optimization_barrier(jnp.mean(shifted * shifted, axis=1, keepdims=True))
    normed = (shifted * lax.rsqrt(mean_square + norm_eps)).astype(jnp.bfloat16)
    projected = jnp.dot(normed, qkv_weight, preferred_element_type=jnp.float32).astype(jnp.bfloat16)
    projected = projected.reshape(TOKENS, 3, HEADS, HEAD_SIZE).transpose(1, 2, 0, 3)
    attended = lax.map(one_head, (projected[0], projected[1], projected[2]))
    attended = attended.transpose(1, 0, 2).reshape(TOKENS, INNER)
    return jnp.dot(attended, out_weight, preferred_element_type=jnp.float32)

def reference(start_state, timesteps, qkv_weight, out_weight):
    time_embed = embed(timesteps, D)
    states = jnp.broadcast_to(start_state[None], (STEPS, TOKENS, D))
    step_scale = 1.0 / STEPS

    def evaluate(pair):
        return drift_of(pair[0], pair[1], qkv_weight, out_weight)
    result = states
    for round_index in range(ITERS):
        drifts = lax.map(evaluate, (states, time_embed))
        inclusive = jnp.cumsum(drifts, axis=0)
        if round_index == ITERS - 1:
            result = start_state[None] + step_scale * inclusive
        else:
            exclusive = jnp.concatenate([jnp.zeros((1, TOKENS, D), jnp.float32), inclusive[:-1]], axis=0)
            states = start_state[None] + step_scale * exclusive
    return result
```

```python
import functools
import math

import jax
import jax.numpy as jnp
from jax import lax
from jax.experimental import pallas as pl
from jax.experimental.pallas import tpu as pltpu
from jax.sharding import PartitionSpec as P

HEAD_SIZE = 128
HEADS = 16
ITERS = 2
NORM_EPS = 1e-06
MESH = pl.DeviceIdType.MESH
F32 = jnp.float32
BF16 = jnp.bfloat16


def embed(step_index, model_width):
    half_width = model_width // 2
    frequency = jnp.exp(-math.log(10000.0) * jnp.arange(half_width, dtype=F32) / half_width)
    angles = step_index.astype(F32)[:, None] * frequency[None, :]
    return jnp.concatenate([jnp.sin(angles), jnp.cos(angles)], axis=1)


def kernel(
    n_step,
    start_ref, te_ref, wqkv_ref, wout_ref,
    out_ref,
    w_ref, wo_ref, x_ref, ns_ref, qkv_ref, att_ref, recv_ref, dr_ref, bs_ref, pr_ref, pe_ref, e_ref, pf_ref, ef_ref,
    w_sem, wo_sem, wo_send, wo_recv, wo_fsend, wo_frecv,
    x_send, x_recv, x_fsend, x_frecv,
    a_sem, a_send, a_recv,
    p_send, p_recv, e_send, e_recv,
):
    tok, width = start_ref.shape
    total_tok = 8 * tok
    group = HEADS // 4
    gw = group * HEAD_SIZE
    inner = HEADS * HEAD_SIZE
    n_total = 2 * n_step
    s = lax.axis_index("step")
    q = lax.axis_index("seq")
    y, c = q // 2, q % 2
    j = y // 2
    g = (y % 2) * 2 + c
    row_parts = min(n_step, 8)
    lane_parts = n_step // row_parts
    prow, plane = tok // row_parts, width // lane_parts
    scale = 1.0 / n_total

    w_copies = []
    for part in range(3):
        w_copies.append(pltpu.make_async_copy(
            wqkv_ref.at[:, pl.ds(pl.multiple_of(part * inner + g * gw, 128), gw)],
            w_ref.at[:, pl.ds(part * gw, gw)],
            w_sem.at[part]))
        w_copies[-1].start()
    orow = wout_ref.shape[0]
    wo_own = pltpu.make_async_copy(
        wout_ref, wo_ref.at[pl.ds(pl.multiple_of(q * orow, orow), orow)], wo_sem)
    wo_own.start()

    barrier = pltpu.get_barrier_semaphore()
    for k in range(1, 8):
        pl.semaphore_signal(barrier, inc=1, device_id=(s, lax.rem(q + k, 8)), device_id_type=MESH)
    for k in range(1, n_step):
        pl.semaphore_signal(barrier, inc=1, device_id=(lax.rem(s + k, n_step), q), device_id_type=MESH)
    pl.semaphore_wait(barrier, 7 + n_step - 1)

    def other(dy):
        return lax.rem(y + dy, 4)

    def wo_rows(ref, qq):
        return ref.at[pl.ds(pl.multiple_of(qq * orow, orow), orow)]

    def wo_copy(dy):
        return pltpu.make_async_remote_copy(
            src_ref=wout_ref, dst_ref=wo_rows(wo_ref, q),
            send_sem=wo_send.at[dy - 1], recv_sem=wo_recv.at[dy - 1],
            device_id=(s, 2 * other(dy) + c), device_id_type=MESH)

    def wo_arrival(dy):
        src = 2 * other(4 - dy) + c
        return pltpu.make_async_remote_copy(
            src_ref=wout_ref, dst_ref=wo_rows(wo_ref, src),
            send_sem=wo_send.at[dy - 1], recv_sem=wo_recv.at[dy - 1],
            device_id=(s, q), device_id_type=MESH)

    def wo_forward(dy):
        src = 2 * other(4 - dy) + c
        return pltpu.make_async_remote_copy(
            src_ref=wo_rows(wo_ref, src), dst_ref=wo_rows(wo_ref, src),
            send_sem=wo_fsend.at[dy % 4], recv_sem=wo_frecv.at[dy % 4],
            device_id=(s, 2 * y + 1 - c), device_id_type=MESH)

    def wo_forwarded(dy):
        src = 2 * other(4 - dy) + 1 - c
        return pltpu.make_async_remote_copy(
            src_ref=wo_rows(wo_ref, src), dst_ref=wo_rows(wo_ref, src),
            send_sem=wo_fsend.at[dy % 4], recv_sem=wo_frecv.at[dy % 4],
            device_id=(s, 2 * y + 1 - c), device_id_type=MESH)

    def x_rows(qq):
        return x_ref.at[pl.ds(pl.multiple_of(qq * tok, tok), tok)]

    def x_copy(dy):
        dest = other(dy)
        return pltpu.make_async_remote_copy(
            src_ref=ns_ref.at[dest // 2], dst_ref=x_rows(q),
            send_sem=x_send.at[dy - 1], recv_sem=x_recv.at[dy - 1],
            device_id=(s, 2 * dest + c), device_id_type=MESH)

    def x_arrival(dy):
        return pltpu.make_async_remote_copy(
            src_ref=ns_ref.at[0], dst_ref=x_rows(2 * other(4 - dy) + c),
            send_sem=x_send.at[dy - 1], recv_sem=x_recv.at[dy - 1],
            device_id=(s, q), device_id_type=MESH)

    def x_forward(dy):
        src = 2 * other(4 - dy) + c
        return pltpu.make_async_remote_copy(
            src_ref=x_rows(src), dst_ref=x_rows(src),
            send_sem=x_fsend.at[dy % 4], recv_sem=x_frecv.at[dy % 4],
            device_id=(s, 2 * y + 1 - c), device_id_type=MESH)

    def x_forwarded(dy):
        src = 2 * other(4 - dy) + 1 - c
        return pltpu.make_async_remote_copy(
            src_ref=x_rows(src), dst_ref=x_rows(src),
            send_sem=x_fsend.at[dy % 4], recv_sem=x_frecv.at[dy % 4],
            device_id=(s, 2 * y + 1 - c), device_id_type=MESH)

    def piece(ref, who):
        return ref.at[pl.ds(pl.multiple_of((who // lane_parts) * prow, prow), prow),
                      pl.ds(pl.multiple_of((who % lane_parts) * plane, 128), plane)]

    def put_normed(i, state):
        shifted = state + te_ref[i:i + 1, :]
        mean_square = jnp.mean(shifted * shifted, axis=1, keepdims=True)
        ns_ref[i] = (shifted * lax.rsqrt(mean_square + NORM_EPS)).astype(BF16)

    def project(yy):
        rows = pl.ds(pl.multiple_of(yy * 2 * tok, 2 * tok), 2 * tok)

        def columns(n, _):
            cols = pl.ds(pl.multiple_of(n * gw, gw), gw)
            factor = jnp.where(n == 0, math.log2(math.e) / math.sqrt(HEAD_SIZE), 1.0)
            qkv_ref[rows, cols] = (jnp.dot(
                x_ref[rows, :], w_ref[:, cols], preferred_element_type=F32) * factor).astype(BF16)
            return 0

        lax.fori_loop(0, 3, columns, 0)

    def attend(yy):
        start_row = pl.multiple_of(yy * 2 * tok, 2 * tok)
        rows = pl.ds(start_row, 2 * tok)

        def head(h, _):
            def cols(part):
                return pl.ds(pl.multiple_of(part * gw + h * HEAD_SIZE, HEAD_SIZE), HEAD_SIZE)

            scores = lax.dot_general(
                qkv_ref[rows, cols(0)], qkv_ref[:, cols(1)],
                (((1,), (1,)), ((), ())), preferred_element_type=F32)
            peak = jnp.max(scores, axis=1, keepdims=True)
            expo = jnp.exp2(scores - peak)
            total = jnp.sum(expo, axis=1, keepdims=True)
            mixed = jnp.dot(expo.astype(BF16), qkv_ref[:, cols(2)], preferred_element_type=F32)
            att_ref[rows, cols(0)] = (mixed / total).astype(BF16)
            return 0

        lax.fori_loop(0, group, head, 0)

    def recv_block(qq):
        yy, cc = qq // 2, qq % 2
        return recv_ref.at[pl.ds(pl.multiple_of((yy // 2) * tok, tok), tok),
                           pl.ds(pl.multiple_of(((yy % 2) * 2 + cc) * gw, gw), gw)]

    def att_rows(qq):
        return att_ref.at[pl.ds(pl.multiple_of(qq * tok, tok), tok)]

    def a_copy(dy, dc):
        dest = 2 * other(dy) + lax.rem(c + dc, 2)
        return pltpu.make_async_remote_copy(
            src_ref=att_rows(dest), dst_ref=recv_block(q),
            send_sem=a_send.at[2 * dy + dc - 1], recv_sem=a_recv.at[2 * dy + dc - 1],
            device_id=(s, dest), device_id_type=MESH)

    def a_arrival(dy, dc):
        src = 2 * other(4 - dy) + lax.rem(c + dc, 2)
        return pltpu.make_async_remote_copy(
            src_ref=att_rows(q), dst_ref=recv_block(src),
            send_sem=a_send.at[2 * dy + dc - 1], recv_sem=a_recv.at[2 * dy + dc - 1],
            device_id=(s, q), device_id_type=MESH)

    def step_peer(k):
        return lax.rem(s + k, n_step)

    for it in range(ITERS):
        if it == 0:
            for i in range(2):
                put_normed(i, start_ref[...])
        else:
            before = e_ref[...].astype(F32)
            put_normed(0, start_ref[...] + scale * before)
            put_normed(1, start_ref[...] + scale * (before + dr_ref[0]))

        for dy in (2, 1, 3):
            x_copy(dy).start()
        x_rows(q)[...] = ns_ref[j]
        x_forward(0).start()
        if it == 0:
            for dy in (2, 1, 3):
                wo_copy(dy).start()
            for copy in w_copies:
                copy.wait()
        x_forwarded(0).wait_recv()
        project(y)
        for dy in (1, 3, 2):
            x_arrival(dy).wait_recv()
            x_forward(dy).start()
            x_forwarded(dy).wait_recv()
            project(other(4 - dy))
        for dy in (1, 2, 3):
            x_copy(dy).wait_send()
        for dy in range(4):
            x_forward(dy).wait_send()

        for dy in (2, 1, 3, 0):
            attend(other(dy))
            for dc in (0, 1):
                if dy == 0 and dc == 0:
                    own = pltpu.make_async_copy(att_rows(q), recv_block(q), a_sem)
                    own.start()
                else:
                    a_copy(dy, dc).start()
        if it == 0:
            wo_own.wait()
            wo_forward(0).start()
            for dy in (1, 3, 2):
                wo_arrival(dy).wait_recv()
                wo_forward(dy).start()
            for dy in range(4):
                wo_forwarded(dy).wait_recv()
            for dy in (1, 2, 3):
                wo_copy(dy).wait_send()
            for dy in range(4):
                wo_forward(dy).wait_send()
        own.wait()
        for n in range(1, 8):
            a_arrival(n // 2, n % 2).wait_recv()
        for n in range(1, 8):
            a_copy(n // 2, n % 2).wait_send()

        def drift(n, _):
            cols = pl.ds(pl.multiple_of(n * 256, 256), 256)
            both = jnp.dot(recv_ref[...], wo_ref[:, cols], preferred_element_type=F32)
            first, second = both[:tok], both[tok:]
            dr_ref[0, :, cols] = first
            dr_ref[1, :, cols] = first + second
            bs_ref[:, cols] = (first + second).astype(BF16)
            return 0

        lax.fori_loop(0, width // 256, drift, 0)

        pieces, sums = (pe_ref, e_ref) if it < ITERS - 1 else (pf_ref, ef_ref)

        def p_copy(k):
            dest = step_peer(k)
            return pltpu.make_async_remote_copy(
                src_ref=piece(bs_ref, dest), dst_ref=pr_ref.at[s],
                send_sem=p_send.at[k - 1], recv_sem=p_recv.at[k - 1],
                device_id=(dest, q), device_id_type=MESH)

        def p_arrival(k):
            return pltpu.make_async_remote_copy(
                src_ref=piece(bs_ref, s), dst_ref=pr_ref.at[step_peer(n_step - k)],
                send_sem=p_send.at[k - 1], recv_sem=p_recv.at[k - 1],
                device_id=(s, q), device_id_type=MESH)

        def e_copy(k):
            dest = step_peer(k)
            return pltpu.make_async_remote_copy(
                src_ref=pieces.at[dest], dst_ref=piece(sums, s),
                send_sem=e_send.at[k - 1], recv_sem=e_recv.at[k - 1],
                device_id=(dest, q), device_id_type=MESH)

        def e_arrival(k):
            return pltpu.make_async_remote_copy(
                src_ref=pieces.at[s], dst_ref=piece(sums, step_peer(n_step - k)),
                send_sem=e_send.at[k - 1], recv_sem=e_recv.at[k - 1],
                device_id=(s, q), device_id_type=MESH)

        for k in range(1, n_step):
            p_copy(k).start()
        pr_ref[s] = piece(bs_ref, s)[...]
        for k in range(1, n_step):
            p_arrival(k).wait_recv()

        def prefix(k, total):
            pieces[k] = total.astype(pieces.dtype)
            return total + pr_ref[k].astype(F32)

        lax.fori_loop(0, n_step, prefix, jnp.zeros((prow, plane), F32))
        for k in range(1, n_step):
            e_copy(k).start()
        piece(sums, s)[...] = pieces[s]
        for k in range(1, n_step):
            e_arrival(k).wait_recv()
        for k in range(1, n_step):
            p_copy(k).wait_send()
            e_copy(k).wait_send()

    before = ef_ref[...]
    for i in range(2):
        out_ref[i] = before + dr_ref[i]


def on_device(n_step, start_state, timesteps, qkv_weight, out_weight):
    tok, width = start_state.shape
    inner = HEADS * HEAD_SIZE
    te = embed(timesteps, width)
    row_parts = min(n_step, 8)
    lane_parts = n_step // row_parts
    prow, plane = tok // row_parts, width // lane_parts
    dma = pltpu.SemaphoreType.DMA
    vmem = pl.BlockSpec(memory_space=pltpu.VMEM)
    hbm = pl.BlockSpec(memory_space=pl.ANY)
    sums = pl.pallas_call(
        functools.partial(kernel, n_step),
        out_shape=jax.ShapeDtypeStruct((2, tok, width), F32),
        in_specs=[vmem, vmem, hbm, vmem],
        out_specs=vmem,
        scratch_shapes=[
            pltpu.VMEM((width, 3 * inner // 4), BF16),
            pltpu.VMEM((inner, width), BF16),
            pltpu.VMEM((8 * tok, width), BF16),
            pltpu.VMEM((2, tok, width), BF16),
            pltpu.VMEM((8 * tok, 3 * inner // 4), BF16),
            pltpu.VMEM((8 * tok, inner // 4), BF16),
            pltpu.VMEM((2 * tok, inner), BF16),
            pltpu.VMEM((2, tok, width), F32),
            pltpu.VMEM((tok, width), BF16),
            pltpu.VMEM((n_step, prow, plane), BF16),
            pltpu.VMEM((n_step, prow, plane), BF16),
            pltpu.VMEM((tok, width), BF16),
            pltpu.VMEM((n_step, prow, plane), F32),
            pltpu.VMEM((tok, width), F32),
            dma((3,)), dma, dma((3,)), dma((3,)), dma((4,)), dma((4,)),
            dma((3,)), dma((3,)), dma((4,)), dma((4,)),
            dma, dma((7,)), dma((7,)),
            dma((n_step - 1,)), dma((n_step - 1,)), dma((n_step - 1,)), dma((n_step - 1,)),
        ],
        compiler_params=pltpu.CompilerParams(
            collective_id=0, has_side_effects=True, vmem_limit_bytes=50 * 1024 * 1024),
        name="picard",
    )(start_state, te, qkv_weight, out_weight)
    return start_state[None] + (1.0 / (2 * n_step)) * sums


def solution(mesh):
    return jax.shard_map(
        functools.partial(on_device, mesh.shape["step"]),
        mesh=mesh,
        in_specs=(P("seq", None), P("step"), P(), P("seq", None)),
        out_specs=P("step", "seq", None),
        check_vma=False,
    )
```

```python
import functools
import math

import jax
import jax.numpy as jnp
from jax import lax
from jax.experimental import pallas as pl
from jax.experimental.pallas import tpu as pltpu
from jax.sharding import PartitionSpec as P

HEAD_SIZE = 128
HEADS = 16
INNER = HEADS * HEAD_SIZE
STEP_DEVS = 16
SEQ_DEVS = 8
STEPS = 32
NORM_EPS = 1e-06
MESH = pl.DeviceIdType.MESH
F32 = jnp.float32
BF16 = jnp.bfloat16
QUERY_SCALE = math.log2(math.e) / math.sqrt(HEAD_SIZE)


def embed(step_index, model_width):
    half_width = model_width // 2
    frequency = jnp.exp(-math.log(10000.0) * jnp.arange(half_width, dtype=F32) / half_width)
    angles = step_index.astype(F32)[:, None] * frequency[None, :]
    return jnp.concatenate([jnp.sin(angles), jnp.cos(angles)], axis=1)


def remote(src, dst, send_sem, recv_sem, device):
    return pltpu.make_async_remote_copy(
        src_ref=src, dst_ref=dst, send_sem=send_sem, recv_sem=recv_sem,
        device_id=device, device_id_type=MESH)


def aligned(value, by):
    return pl.multiple_of(value, by)


def each(first, last, body):
    def step(k, carry):
        body(k)
        return carry

    lax.fori_loop(first, last, step, 0)


def split_dot(values, weights):
    high = values.astype(BF16)
    low = (values - high.astype(F32)).astype(BF16)
    return (jnp.dot(high, weights, preferred_element_type=F32)
            + jnp.dot(low, weights, preferred_element_type=F32))


def softmax_mix(queries, keys, values):
    scores = lax.dot_general(queries, keys, (((1,), (1,)), ((), ())), preferred_element_type=F32)
    expo = jnp.exp2(scores - jnp.max(scores, axis=1, keepdims=True))
    total = jnp.sum(expo, axis=1, keepdims=True)
    mixed = jnp.dot(expo.astype(BF16), values, preferred_element_type=F32)
    return (mixed / total).astype(BF16)


def kernel(
    te_ref, start_ref, wqkv_ref, wout_ref,
    out_ref,
    w1, w2, wo, st, tea, tes, swb, rtb, tew, qkv1, att1, recv1, dr1, bs1, pr1, pe1, e1, stb, ns,
    xs, qkv2, att2, recv2, dr2, bs2, pr2, pe2, e2,
    w1_sem, w2_sem, wo_sem, st_sem,
    te_send, te_recv, sw_send, sw_recv, swf_send, swf_recv, rt_send, rt_recv, sb_send, sb_recv,
    wy_send, wy_recv, wz_send, wz_recv, wf_send, wf_recv,
    a1_send, a1_recv, p1_send, p1_recv, e1_send, e1_recv,
    x_send, x_recv, xf_send, xf_recv,
    a2_send, a2_recv, a2_sem, p2_send, p2_recv, e2_send, e2_recv,
):
    tok, width = start_ref.shape
    half, part = tok // 2, tok // 4
    lane4 = width // 4
    orow = wout_ref.shape[0]
    s = lax.axis_index("step")
    q = lax.axis_index("seq")
    y, c = q // 2, q % 2
    parity = y // 2
    group = (y % 2) * 2 + c
    gw = INNER // 4
    scale = 1.0 / STEPS
    here = (s, q)
    mate = (s, 2 * y + 1 - c)

    def chip(dy):
        return lax.rem(y + dy, 4)

    def step_peer(k):
        return lax.rem(s + k, STEP_DEVS)

    def seq_peer(k):
        return lax.rem(q + k, SEQ_DEVS)

    def w1_copy(n):
        return pltpu.make_async_copy(
            wqkv_ref.at[:, pl.ds(aligned(n * INNER + s * HEAD_SIZE, 128), HEAD_SIZE)],
            w1.at[:, pl.ds(n * HEAD_SIZE, HEAD_SIZE)], w1_sem.at[n])

    def w2_copy(n):
        return pltpu.make_async_copy(
            wqkv_ref.at[:, pl.ds(aligned(n * INNER + group * gw, 128), gw)],
            w2.at[:, pl.ds(n * gw, gw)], w2_sem.at[n])

    def st_copy(n):
        h, b = n // 2, n % 2
        return pltpu.make_async_copy(
            start_ref.at[pl.ds(half * b + part * h, part)],
            st.at[pl.ds(half * h + part * b, part)], st_sem.at[n])

    def wo_rows(owner, first, count):
        return wo.at[pl.ds(aligned(owner * orow + first, 16), count)]

    wo_own = pltpu.make_async_copy(wout_ref, wo_rows(q, 0, orow), wo_sem)
    for n in range(4):
        st_copy(n).start()
    for n in range(3):
        w1_copy(n).start()
    wo_own.start()

    barrier = pltpu.get_barrier_semaphore()
    for k in range(1, STEP_DEVS):
        pl.semaphore_signal(barrier, inc=1, device_id=(step_peer(k), q), device_id_type=MESH)
    for k in range(1, SEQ_DEVS):
        pl.semaphore_signal(barrier, inc=1, device_id=(s, seq_peer(k)), device_id_type=MESH)
    pl.semaphore_wait(barrier, STEP_DEVS - 1 + SEQ_DEVS - 1)

    def te_copy(k):
        return remote(te_ref, tea.at[s], te_send.at[k - 1], te_recv.at[k - 1], (step_peer(k), q))

    def te_arrival(k):
        return remote(te_ref, tea.at[step_peer(STEP_DEVS - k)], te_send.at[k - 1], te_recv.at[k - 1], here)

    each(1, STEP_DEVS, lambda k: te_copy(k).start())
    tea[s] = te_ref[...]

    for n in range(4):
        st_copy(n).wait()
    for n in range(3):
        w1_copy(n).wait()
    lane = lax.broadcasted_iota(jnp.int32, (1, 3 * HEAD_SIZE), 1)
    factor = jnp.where(lane < HEAD_SIZE, QUERY_SCALE, 1.0)
    swb[q] = (split_dot(st[...], w1[...]) * factor).astype(BF16)

    def sw_copy(dy):
        return remote(swb.at[q], swb.at[q], sw_send.at[dy - 1], sw_recv.at[dy - 1], (s, 2 * chip(dy) + c))

    def sw_arrival(dy):
        return remote(swb.at[q], swb.at[2 * chip(4 - dy) + c], sw_send.at[dy - 1], sw_recv.at[dy - 1], here)

    def sw_forward(dy):
        owner = 2 * chip(4 - dy) + c
        return remote(swb.at[owner], swb.at[owner], swf_send.at[dy % 4], swf_recv.at[dy % 4], mate)

    def sw_forwarded(dy):
        owner = 2 * chip(4 - dy) + 1 - c
        return remote(swb.at[owner], swb.at[owner], swf_send.at[dy % 4], swf_recv.at[dy % 4], mate)

    for dy in (2, 1, 3):
        sw_copy(dy).start()
    sw_forward(0).start()

    zp = (s // 4) % 2

    def wy_copy(dy):
        return remote(wout_ref.at[pl.ds(aligned(zp * (orow // 2), 16), orow // 2)],
                      wo_rows(q, zp * (orow // 2), orow // 2),
                      wy_send.at[dy - 1], wy_recv.at[dy - 1], (s, 2 * chip(dy) + c))

    def wy_arrival(dy):
        rows = wo_rows(2 * chip(4 - dy) + c, zp * (orow // 2), orow // 2)
        return remote(rows, rows, wy_send.at[dy - 1], wy_recv.at[dy - 1], here)

    def wz_copy(dy, up):
        rows = wo_rows(2 * chip(4 - dy) + c, zp * (orow // 2) + up * (orow // 4), orow // 4)
        return remote(rows, rows, wz_send.at[2 * dy - 2 + up], wz_recv.at[2 * dy - 2 + up],
                      (step_peer(4 if up else STEP_DEVS - 4), q))

    def wz_arrival(dy, up):
        rows = wo_rows(2 * chip(4 - dy) + c, (1 - zp) * (orow // 2) + up * (orow // 4), orow // 4)
        return remote(rows, rows, wz_send.at[2 * dy - 2 + up], wz_recv.at[2 * dy - 2 + up], here)

    def wf_rows(n, core):
        if n == 0:
            return wo_rows(2 * y + core, 0, orow)
        dy, kind = (n - 1) // 3 + 1, (n - 1) % 3
        owner = 2 * chip(4 - dy) + core
        if kind == 0:
            return wo_rows(owner, zp * (orow // 2), orow // 2)
        return wo_rows(owner, (1 - zp) * (orow // 2) + (kind - 1) * (orow // 4), orow // 4)

    def wf_copy(n):
        return remote(wf_rows(n, c), wf_rows(n, c), wf_send.at[n], wf_recv.at[n], mate)

    def wf_arrival(n):
        return remote(wf_rows(n, 1 - c), wf_rows(n, 1 - c), wf_send.at[n], wf_recv.at[n], mate)

    for dy in (2, 1, 3):
        wy_copy(dy).start()

    owner_q = s // 2
    block = s % 2

    def sb_src(h):
        return st.at[pl.ds(aligned(half * h + part * block, 8), part)]

    def sb_copy(k, h):
        return remote(sb_src(h), stb.at[h], sb_send.at[h, k - 1], sb_recv.at[h], (s, seq_peer(k)))

    @pl.when(q == owner_q)
    def _():
        for h in range(2):
            each(1, SEQ_DEVS, lambda k: sb_copy(k, h).start())
            stb[h] = sb_src(h)[...]

    for n in range(3):
        w2_copy(n).start()

    each(1, STEP_DEVS, lambda k: te_arrival(k).wait_recv())
    for n in range(STEP_DEVS):
        tes[2 * n:2 * n + 2, :] = tea[n]
    own = st[...]
    cross = lax.dot_general(tes[...], own, (((1,), (1,)), ((), ())),
                            precision=lax.Precision.HIGHEST, preferred_element_type=F32)
    squares = lax.dot_general(jnp.ones((8, width), F32), own * own, (((1,), (1,)), ((), ())),
                              precision=lax.Precision.HIGHEST, preferred_element_type=F32)[0:1]
    step_squares = jnp.sum(tes[...] * tes[...], axis=1, keepdims=True)
    mean_square = jnp.maximum((squares + 2.0 * cross + step_squares) * (1.0 / width), 0.0)
    rtb[q] = lax.rsqrt(mean_square + NORM_EPS)

    def rt_copy(k):
        return remote(rtb.at[q], rtb.at[q], rt_send.at[k - 1], rt_recv.at[k - 1], (s, seq_peer(k)))

    def rt_arrival(k):
        return remote(rtb.at[q], rtb.at[seq_peer(SEQ_DEVS - k)], rt_send.at[k - 1], rt_recv.at[k - 1], here)

    each(1, SEQ_DEVS, lambda k: rt_copy(k).start())
    tew[...] = split_dot(tes[...], w1[...]) * factor

    for dy in (1, 3, 2):
        sw_arrival(dy).wait_recv()
        sw_forward(dy).start()
    each(1, SEQ_DEVS, lambda k: rt_arrival(k).wait_recv())
    for dy in range(4):
        sw_forwarded(dy).wait_recv()

    def build(n):
        i, b = n // SEQ_DEVS, lax.rem(n, SEQ_DEVS)
        k = 4 * q + i
        pick = (lax.broadcasted_iota(jnp.int32, (STEPS, HEAD_SIZE), 0) == k).astype(F32)
        rows = lax.dot_general(rtb[b], pick, (((0,), (0,)), ((), ())),
                               precision=lax.Precision.HIGHEST, preferred_element_type=F32)
        step_row = tew[pl.ds(k, 1), :]
        for n3 in range(3):
            cols = slice(n3 * HEAD_SIZE, (n3 + 1) * HEAD_SIZE)
            qkv1[i, b, :, cols] = ((swb[b, :, cols].astype(F32) + step_row[:, cols]) * rows).astype(BF16)

    each(0, 4 * SEQ_DEVS, build)

    def a1_copy(h, k):
        return remote(att1.at[h, step_peer(k)], recv1.at[h, :, pl.ds(aligned(s * HEAD_SIZE, 128), HEAD_SIZE)],
                      a1_send.at[h, k - 1], a1_recv.at[h, k - 1], (step_peer(k), q))

    def a1_arrival(h, k):
        src = step_peer(STEP_DEVS - k)
        return remote(att1.at[h, s], recv1.at[h, :, pl.ds(aligned(src * HEAD_SIZE, 128), HEAD_SIZE)],
                      a1_send.at[h, k - 1], a1_recv.at[h, k - 1], here)

    for h in range(2):
        def attend1(n):
            i, sub = n // 2, lax.rem(n, 2)
            queries = qkv1[i, pl.ds(4 * sub, 4), half * h:half * (h + 1), 0:HEAD_SIZE].reshape(4 * half, HEAD_SIZE)
            keys = qkv1[i, :, :, HEAD_SIZE:2 * HEAD_SIZE].reshape(8 * tok, HEAD_SIZE)
            values = qkv1[i, :, :, 2 * HEAD_SIZE:3 * HEAD_SIZE].reshape(8 * tok, HEAD_SIZE)
            mixed = softmax_mix(queries, keys, values).reshape(8, part, HEAD_SIZE)
            att1[h, pl.ds(8 * sub, 8), pl.ds(aligned(i * part, part), part), :] = mixed

        each(0, 8, attend1)
        each(1, STEP_DEVS, lambda k: a1_copy(h, k).start())
        recv1[h, :, pl.ds(aligned(s * HEAD_SIZE, 128), HEAD_SIZE)] = att1[h, s]
        if h == 0:
            wo_own.wait()
            wf_copy(0).start()
            for dy in (1, 3, 2):
                wy_arrival(dy).wait_recv()
                wz_copy(dy, 0).start()
                wz_copy(dy, 1).start()
                wf_copy(3 * dy - 2).start()
        else:
            for dy in (1, 3, 2):
                for up in range(2):
                    wz_arrival(dy, up).wait_recv()
                    wf_copy(3 * dy - 1 + up).start()
    for n in range(10):
        wf_arrival(n).wait_recv()

    def piece(ref, who):
        return ref.at[pl.ds(aligned((who // 4) * 16, 16), 16), pl.ds(aligned((who % 4) * lane4, 128), lane4)]

    def p1_copy(h, k):
        dest = seq_peer(k)
        return remote(piece(bs1.at[h], dest), pr1.at[h, q], p1_send.at[h, k - 1], p1_recv.at[h, k - 1], (s, dest))

    def p1_arrival(h, k):
        return remote(piece(bs1.at[h], q), pr1.at[h, seq_peer(SEQ_DEVS - k)],
                      p1_send.at[h, k - 1], p1_recv.at[h, k - 1], here)

    def e1_copy(h, k):
        dest = seq_peer(k)
        return remote(pe1.at[h, dest], piece(e1.at[h], q), e1_send.at[h, k - 1], e1_recv.at[h, k - 1], (s, dest))

    def e1_arrival(h, k):
        return remote(pe1.at[h, q], piece(e1.at[h], seq_peer(SEQ_DEVS - k)),
                      e1_send.at[h, k - 1], e1_recv.at[h, k - 1], here)

    def drift1(h):
        each(1, STEP_DEVS, lambda k: a1_arrival(h, k).wait_recv())

        def tile(n):
            cols = pl.ds(aligned(n * 256, 256), 256)
            rows = jnp.dot(recv1[h], wo[:, cols], preferred_element_type=F32)
            total = rows[0:part]
            dr1[h, 0, :, cols] = total
            for i in range(1, 4):
                total = total + rows[i * part:(i + 1) * part]
                dr1[h, i, :, cols] = total
            bs1[h, :, cols] = total.astype(BF16)

        each(0, width // 256, tile)
        each(1, SEQ_DEVS, lambda k: p1_copy(h, k).start())
        pr1[h, q] = piece(bs1.at[h], q)[...]

    def scan1(h):
        each(1, SEQ_DEVS, lambda k: p1_arrival(h, k).wait_recv())
        total = jnp.zeros((16, lane4), F32)
        for k in range(SEQ_DEVS):
            pe1[h, k] = total.astype(BF16)
            total = total + pr1[h, k].astype(F32)
        each(1, SEQ_DEVS, lambda k: e1_copy(h, k).start())
        piece(e1.at[h], q)[...] = pe1[h, q]

    def x_rows(h, who):
        return xs.at[pl.ds(aligned(h * 8 * half + who * part, part), part)]

    def x_target(h, n):
        i, e = n // 2, n % 2
        return 2 * q + i // 2, 2 * (2 * (i % 2) + e) + lax.rem(s + h, 2)

    def x_copy(h, n):
        return remote(ns.at[h, n // 2], x_rows(h, s), x_send.at[h, n], x_recv.at[h, s // 2], x_target(h, n))

    def is_here(h, n):
        a, b = x_target(h, n)
        return jnp.logical_and(a == s, b == q)

    def x_local(h, n):
        return pltpu.make_async_copy(ns.at[h, n // 2], x_rows(h, s), x_recv.at[h, s // 2])

    def direct(h, m):
        return 2 * m + lax.rem(c + h, 2)

    def x_arrival(h, m):
        rows = x_rows(h, direct(h, m))
        return pltpu.make_async_copy(rows, rows, x_recv.at[h, m])

    def x_forward(h, m):
        rows = x_rows(h, direct(h, m))
        return remote(rows, rows, xf_send.at[h, m], xf_recv.at[h, m], mate)

    def x_forwarded(h, m):
        rows = x_rows(h, 2 * m + lax.rem(c + h + 1, 2))
        return remote(rows, rows, xf_send.at[h, m], xf_recv.at[h, m], mate)

    def states(h):
        each(1, SEQ_DEVS, lambda k: e1_arrival(h, k).wait_recv())
        for i in range(4):
            before = e1[h].astype(F32)
            if i:
                before = before + dr1[h, i - 1]
            shifted = stb[h] + scale * before + tes[pl.ds(4 * q + i, 1), :]
            mean = jnp.mean(shifted * shifted, axis=1, keepdims=True)
            ns[h, i] = (shifted * lax.rsqrt(mean + NORM_EPS)).astype(BF16)
            for n in (2 * i, 2 * i + 1):
                @pl.when(is_here(h, n))
                def _():
                    x_local(h, n).start()

                @pl.when(jnp.logical_not(is_here(h, n)))
                def _():
                    x_copy(h, n).start()

    @pl.when(q != owner_q)
    def _():
        for h in range(2):
            sb_copy_in = remote(stb.at[h], stb.at[h], sb_send.at[h, 0], sb_recv.at[h], here)
            sb_copy_in.wait_recv()

    drift1(0)
    scan1(0)
    drift1(1)
    states(0)
    scan1(1)
    states(1)

    for n in range(3):
        w2_copy(n).wait()

    def project(h, sub):
        rows = pl.ds(h * 8 * half + sub * 4 * half, 4 * half)

        def columns(n):
            cols = pl.ds(aligned(n * gw, gw), gw)
            f = jnp.where(n == 0, QUERY_SCALE, 1.0)
            qkv2[rows, cols] = (jnp.dot(xs[rows, :], w2[:, cols], preferred_element_type=F32) * f).astype(BF16)

        each(0, 3, columns)

    for h in range(2):
        for sub in range(2):
            for m in range(4 * sub, 4 * sub + 4):
                x_arrival(h, m).wait()
                x_forward(h, m).start()
        for sub in range(2):
            for m in range(4 * sub, 4 * sub + 4):
                x_forwarded(h, m).wait_recv()
            project(h, sub)

    def a2_block(h, who):
        yy, cc = who // 2, who % 2
        return recv2.at[h, pl.ds(aligned((yy // 2) * half, half), half),
                        pl.ds(aligned(((yy % 2) * 2 + cc) * gw, gw), gw)]

    def att2_rows(h, who):
        return att2.at[pl.ds(aligned(h * 8 * half + who * half, half), half)]

    def a2_copy(h, k):
        dest = seq_peer(k)
        return remote(att2_rows(h, dest), a2_block(h, q), a2_send.at[h, k - 1], a2_recv.at[h, k - 1], (s, dest))

    def a2_arrival(h, k):
        return remote(att2_rows(h, q), a2_block(h, seq_peer(SEQ_DEVS - k)),
                      a2_send.at[h, k - 1], a2_recv.at[h, k - 1], here)

    def a2_own(h):
        return pltpu.make_async_copy(att2_rows(h, q), a2_block(h, q), a2_sem.at[h])

    for h in range(2):
        def attend2(n):
            sub, head = n // 4, lax.rem(n, 4)
            rows = pl.ds(aligned(h * 8 * half + sub * 4 * half, 4 * half), 4 * half)

            def cols(p):
                return pl.ds(aligned(p * gw + head * HEAD_SIZE, HEAD_SIZE), HEAD_SIZE)

            att2[rows, cols(0)] = softmax_mix(qkv2[rows, cols(0)], qkv2[:, cols(1)], qkv2[:, cols(2)])

        each(0, 8, attend2)
        each(1, SEQ_DEVS, lambda k: a2_copy(h, k).start())
        a2_own(h).start()

    def p2_copy(h, k):
        dest = step_peer(k)
        return remote(piece(bs2.at[h], dest), pr2.at[h, s], p2_send.at[h, k - 1], p2_recv.at[h, k - 1], (dest, q))

    def p2_arrival(h, k):
        return remote(piece(bs2.at[h], s), pr2.at[h, step_peer(STEP_DEVS - k)],
                      p2_send.at[h, k - 1], p2_recv.at[h, k - 1], here)

    def e2_copy(h, k):
        dest = step_peer(k)
        return remote(pe2.at[h, dest], piece(e2.at[h], s), e2_send.at[h, k - 1], e2_recv.at[h, k - 1], (dest, q))

    def e2_arrival(h, k):
        return remote(pe2.at[h, s], piece(e2.at[h], step_peer(STEP_DEVS - k)),
                      e2_send.at[h, k - 1], e2_recv.at[h, k - 1], here)

    def drift2(h):
        a2_own(h).wait()
        each(1, SEQ_DEVS, lambda k: a2_arrival(h, k).wait_recv())

        def tile(n):
            cols = pl.ds(aligned(n * 256, 256), 256)
            rows = jnp.dot(recv2[h], wo[:, cols], preferred_element_type=F32)
            first = rows[0:half]
            total = first + rows[half:]
            dr2[h, 0, :, cols] = first
            dr2[h, 1, :, cols] = total
            bs2[h, :, cols] = total.astype(BF16)

        each(0, width // 256, tile)
        each(1, STEP_DEVS, lambda k: p2_copy(h, k).start())
        pr2[h, s] = piece(bs2.at[h], s)[...]

    def scan2(h):
        each(1, STEP_DEVS, lambda k: p2_arrival(h, k).wait_recv())
        total = jnp.zeros((16, lane4), F32)
        for k in range(STEP_DEVS):
            pe2[h, k] = total
            total = total + pr2[h, k].astype(F32)
        each(1, STEP_DEVS, lambda k: e2_copy(h, k).start())
        piece(e2.at[h], s)[...] = pe2[h, s]

    def finish(h):
        each(1, STEP_DEVS, lambda k: e2_arrival(h, k).wait_recv())
        for i in range(2):
            for b in range(2):
                rows = slice(part * b, part * (b + 1))
                out_ref[i, half * b + part * h:half * b + part * (h + 1), :] = e2[h, rows, :] + dr2[h, i, rows, :]

    drift2(0)
    scan2(0)
    drift2(1)
    scan2(1)
    finish(0)
    finish(1)

    each(1, STEP_DEVS, lambda k: te_copy(k).wait_send())
    for dy in range(1, 4):
        sw_copy(dy).wait_send()
        wy_copy(dy).wait_send()
        for up in range(2):
            wz_copy(dy, up).wait_send()
    for dy in range(4):
        sw_forward(dy).wait_send()
    for n in range(10):
        wf_copy(n).wait_send()
    each(1, SEQ_DEVS, lambda k: rt_copy(k).wait_send())

    @pl.when(q == owner_q)
    def _():
        for h in range(2):
            each(1, SEQ_DEVS, lambda k: sb_copy(k, h).wait_send())

    for h in range(2):
        for k in range(1, SEQ_DEVS):
            p1_copy(h, k).wait_send()
            e1_copy(h, k).wait_send()
            a2_copy(h, k).wait_send()
        for k in range(1, STEP_DEVS):
            a1_copy(h, k).wait_send()
            p2_copy(h, k).wait_send()
            e2_copy(h, k).wait_send()
        for n in range(8):
            @pl.when(jnp.logical_not(is_here(h, n)))
            def _():
                x_copy(h, n).wait_send()
        for m in range(8):
            x_forward(h, m).wait_send()


def on_device(start_state, timesteps, qkv_weight, out_weight):
    tok, width = start_state.shape
    half, part, lane4 = tok // 2, tok // 4, width // 4
    te = embed(timesteps, width)
    dma = pltpu.SemaphoreType.DMA
    vmem = pl.BlockSpec(memory_space=pltpu.VMEM)
    hbm = pl.BlockSpec(memory_space=pl.ANY)
    sums = pl.pallas_call(
        kernel,
        out_shape=jax.ShapeDtypeStruct((2, tok, width), F32),
        in_specs=[vmem, hbm, hbm, hbm],
        out_specs=vmem,
        scratch_shapes=[
            pltpu.VMEM((width, 3 * HEAD_SIZE), BF16),
            pltpu.VMEM((width, 3 * INNER // 4), BF16),
            pltpu.VMEM((INNER, width), BF16),
            pltpu.VMEM((tok, width), F32),
            pltpu.VMEM((STEP_DEVS, 2, width), F32),
            pltpu.VMEM((STEPS, width), F32),
            pltpu.VMEM((SEQ_DEVS, tok, 3 * HEAD_SIZE), BF16),
            pltpu.VMEM((SEQ_DEVS, STEPS, tok), F32),
            pltpu.VMEM((STEPS, 3 * HEAD_SIZE), F32),
            pltpu.VMEM((4, SEQ_DEVS, tok, 3 * HEAD_SIZE), BF16),
            pltpu.VMEM((2, STEP_DEVS, 4 * part, HEAD_SIZE), BF16),
            pltpu.VMEM((2, 4 * part, INNER), BF16),
            pltpu.VMEM((2, 4, part, width), F32),
            pltpu.VMEM((2, part, width), BF16),
            pltpu.VMEM((2, SEQ_DEVS, 16, lane4), BF16),
            pltpu.VMEM((2, SEQ_DEVS, 16, lane4), BF16),
            pltpu.VMEM((2, part, width), BF16),
            pltpu.VMEM((2, part, width), F32),
            pltpu.VMEM((2, 4, part, width), BF16),
            pltpu.VMEM((8 * tok, width), BF16),
            pltpu.VMEM((8 * tok, 3 * INNER // 4), BF16),
            pltpu.VMEM((8 * tok, INNER // 4), BF16),
            pltpu.VMEM((2, tok, INNER), BF16),
            pltpu.VMEM((2, 2, half, width), F32),
            pltpu.VMEM((2, half, width), BF16),
            pltpu.VMEM((2, STEP_DEVS, 16, lane4), BF16),
            pltpu.VMEM((2, STEP_DEVS, 16, lane4), F32),
            pltpu.VMEM((2, half, width), F32),
            dma((3,)), dma((3,)), dma, dma((4,)),
            dma((15,)), dma((15,)), dma((3,)), dma((3,)), dma((4,)), dma((4,)), dma((7,)), dma((7,)),
            dma((2, 7)), dma((2,)),
            dma((3,)), dma((3,)), dma((6,)), dma((6,)), dma((10,)), dma((10,)),
            dma((2, 15)), dma((2, 15)), dma((2, 7)), dma((2, 7)), dma((2, 7)), dma((2, 7)),
            dma((2, 8)), dma((2, 8)), dma((2, 8)), dma((2, 8)),
            dma((2, 7)), dma((2, 7)), dma((2,)), dma((2, 15)), dma((2, 15)), dma((2, 15)), dma((2, 15)),
        ],
        compiler_params=pltpu.CompilerParams(
            collective_id=0, has_side_effects=True, vmem_limit_bytes=58 * 1024 * 1024),
        name="picard",
    )(te, start_state, qkv_weight, out_weight)
    return start_state[None] + (1.0 / STEPS) * sums


def solution(mesh):
    return jax.shard_map(
        on_device,
        mesh=mesh,
        in_specs=(P("seq", None), P("step"), P(), P("seq", None)),
        out_specs=P("step", "seq", None),
        check_vma=False,
    )
```

```python
import functools
import math

import jax
import jax.numpy as jnp
from jax import lax
from jax.experimental import pallas as pl
from jax.experimental.pallas import tpu as pltpu
from jax.sharding import PartitionSpec as P

HEAD_SIZE = 128
HEADS = 16
INNER = HEADS * HEAD_SIZE
STEP_DEVS = 16
SEQ_DEVS = 8
STEPS = 32
NORM_EPS = 1e-06
MESH = pl.DeviceIdType.MESH
F32 = jnp.float32
BF16 = jnp.bfloat16
QUERY_SCALE = math.log2(math.e) / math.sqrt(HEAD_SIZE)


def embed(step_index, model_width):
    half_width = model_width // 2
    frequency = jnp.exp(-math.log(10000.0) * jnp.arange(half_width, dtype=F32) / half_width)
    angles = step_index.astype(F32)[:, None] * frequency[None, :]
    return jnp.concatenate([jnp.sin(angles), jnp.cos(angles)], axis=1)


def remote(src, dst, send_sem, recv_sem, device):
    return pltpu.make_async_remote_copy(
        src_ref=src, dst_ref=dst, send_sem=send_sem, recv_sem=recv_sem,
        device_id=device, device_id_type=MESH)


def aligned(value, by):
    return pl.multiple_of(value, by)


def each(first, last, body):
    def step(k, carry):
        body(k)
        return carry

    lax.fori_loop(first, last, step, 0)


def split_dot(values, weights):
    high = values.astype(BF16)
    low = (values - high.astype(F32)).astype(BF16)
    return (jnp.dot(high, weights, preferred_element_type=F32)
            + jnp.dot(low, weights, preferred_element_type=F32))


def softmax_mix(queries, keys, values):
    scores = lax.dot_general(queries, keys, (((1,), (1,)), ((), ())), preferred_element_type=F32)
    expo = jnp.exp2(scores - jnp.max(scores, axis=1, keepdims=True))
    total = jnp.sum(expo, axis=1, keepdims=True)
    mixed = jnp.dot(expo.astype(BF16), values, preferred_element_type=F32)
    return (mixed / total).astype(BF16)


def kernel(
    te_ref, start_ref, wqkv_ref, wout_ref,
    out_ref,
    w1, w2, wo, st, tea, tes, swb, rtb, tew, qkv1, att1, recv1, dr1, bs1, pr1, pe1, e1, stb, ns,
    xs, qkv2, att2, recv2, dr2, bs2, pr2, pe2, e2,
    w1_sem, w2_sem, wo_sem, st_sem,
    te_send, te_recv, sw_send, sw_recv, swf_send, swf_recv, rt_send, rt_recv, sb_send, sb_recv,
    wy_send, wy_recv, wr_send, wr_recv, wn_send, wn_recv, wf_send, wf_recv,
    a1_send, a1_recv, p1_send, p1_recv, e1_send, e1_recv,
    x_send, x_recv, xf_send, xf_recv,
    a2_send, a2_recv, a2_sem, p2_send, p2_recv, e2_send, e2_recv,
):
    tok, width = start_ref.shape
    half, part = tok // 2, tok // 4
    lane4 = width // 4
    orow = wout_ref.shape[0]
    s = lax.axis_index("step")
    q = lax.axis_index("seq")
    y, c = q // 2, q % 2
    parity = y // 2
    group = (y % 2) * 2 + c
    gw = INNER // 4
    scale = 1.0 / STEPS
    here = (s, q)
    mate = (s, 2 * y + 1 - c)

    def chip(dy):
        return lax.rem(y + dy, 4)

    def step_peer(k):
        return lax.rem(s + k, STEP_DEVS)

    def seq_peer(k):
        return lax.rem(q + k, SEQ_DEVS)

    def w1_copy(n):
        return pltpu.make_async_copy(
            wqkv_ref.at[:, pl.ds(aligned(n * INNER + s * HEAD_SIZE, 128), HEAD_SIZE)],
            w1.at[:, pl.ds(n * HEAD_SIZE, HEAD_SIZE)], w1_sem.at[n])

    def w2_copy(n):
        return pltpu.make_async_copy(
            wqkv_ref.at[:, pl.ds(aligned(n * INNER + group * gw, 128), gw)],
            w2.at[:, pl.ds(n * gw, gw)], w2_sem.at[n])

    def st_copy(n):
        h, b = n // 2, n % 2
        return pltpu.make_async_copy(
            start_ref.at[pl.ds(half * b + part * h, part)],
            st.at[pl.ds(half * h + part * b, part)], st_sem.at[n])

    def wo_rows(owner, first, count):
        return wo.at[pl.ds(aligned(owner * orow + first, 16), count)]

    wo_own = pltpu.make_async_copy(wout_ref, wo_rows(q, 0, orow), wo_sem)
    for n in range(4):
        st_copy(n).start()
    for n in range(3):
        w1_copy(n).start()
    wo_own.start()

    barrier = pltpu.get_barrier_semaphore()
    each(1, STEP_DEVS, lambda k: pl.semaphore_signal(
        barrier, inc=1, device_id=(step_peer(k), q), device_id_type=MESH))
    each(1, SEQ_DEVS, lambda k: pl.semaphore_signal(
        barrier, inc=1, device_id=(s, seq_peer(k)), device_id_type=MESH))

    for n in range(4):
        st_copy(n).wait()
    for n in range(3):
        w1_copy(n).wait()
    lane = lax.broadcasted_iota(jnp.int32, (1, 3 * HEAD_SIZE), 1)
    factor = jnp.where(lane < HEAD_SIZE, QUERY_SCALE, 1.0)
    swb[q] = (split_dot(st[...], w1[...]) * factor).astype(BF16)
    pl.semaphore_wait(barrier, STEP_DEVS - 1 + SEQ_DEVS - 1)

    def te_copy(k):
        return remote(te_ref, tea.at[s], te_send.at[k - 1], te_recv.at[k - 1], (step_peer(k), q))

    def te_arrival(k):
        return remote(te_ref, tea.at[step_peer(STEP_DEVS - k)], te_send.at[k - 1], te_recv.at[k - 1], here)

    each(1, STEP_DEVS, lambda k: te_copy(k).start())
    tea[s] = te_ref[...]

    def sw_copy(dy):
        return remote(swb.at[q], swb.at[q], sw_send.at[dy - 1], sw_recv.at[dy - 1], (s, 2 * chip(dy) + c))

    def sw_arrival(dy):
        return remote(swb.at[q], swb.at[2 * chip(4 - dy) + c], sw_send.at[dy - 1], sw_recv.at[dy - 1], here)

    def sw_forward(dy):
        owner = 2 * chip(4 - dy) + c
        return remote(swb.at[owner], swb.at[owner], swf_send.at[dy % 4], swf_recv.at[dy % 4], mate)

    def sw_forwarded(dy):
        owner = 2 * chip(4 - dy) + 1 - c
        return remote(swb.at[owner], swb.at[owner], swf_send.at[dy % 4], swf_recv.at[dy % 4], mate)

    for dy in (2, 1, 3):
        sw_copy(dy).start()
    sw_forward(0).start()

    zx = (s // 4 + s) % 2
    hrow, qrow, erow = orow // 2, orow // 4, orow // 8

    def wo_of(n, core, first, count):
        return wo_rows(2 * chip(n) + core, first, count)

    def wy_copy(dy):
        return remote(wout_ref.at[pl.ds(aligned(zx * hrow, 16), hrow)], wo_rows(q, zx * hrow, hrow),
                      wy_send.at[dy - 1], wy_recv.at[dy - 1], (s, 2 * chip(dy) + c))

    def wy_arrival(dy):
        rows = wo_of(4 - dy, c, zx * hrow, hrow)
        return remote(rows, rows, wy_send.at[dy - 1], wy_recv.at[dy - 1], here)

    def wr_copy(r):
        rows = wo_of(1 if r else 3, c, zx * hrow + r * qrow, qrow)
        return remote(rows, rows, wr_send.at[r], wr_recv.at[r], (s, 2 * chip(3 if r else 1) + c))

    def wr_arrival(r):
        rows = wo_of(2, c, zx * hrow + r * qrow, qrow)
        return remote(rows, rows, wr_send.at[r], wr_recv.at[r], here)

    def neighbour(n):
        if n < 2:
            return step_peer(4 if n == 0 else STEP_DEVS - 4)
        return (s // 4) * 4 + lax.rem(s + (1 if n == 2 else 3), 4)

    def wn_copy(b, n):
        rows = wo_of(b, c, zx * hrow + n * erow, erow)
        return remote(rows, rows, wn_send.at[b - 1, n], wn_recv.at[b - 1, n], (neighbour(n), q))

    def wn_arrival(b, n):
        rows = wo_of(b, c, (1 - zx) * hrow + n * erow, erow)
        return remote(rows, rows, wn_send.at[b - 1, n], wn_recv.at[b - 1, n], here)

    def wf_rows(n, core):
        if n == 0:
            return wo_rows(2 * y + core, 0, orow)
        if n < 3:
            return wo_of(1 if n == 1 else 3, core, zx * hrow, hrow)
        if n < 5:
            return wo_of(2, core, zx * hrow + (n - 3) * qrow, qrow)
        return wo_of(n - 4, core, (1 - zx) * hrow, hrow)

    def wf_copy(n):
        return remote(wf_rows(n, c), wf_rows(n, c), wf_send.at[n], wf_recv.at[n], mate)

    def wf_arrival(n):
        return remote(wf_rows(n, 1 - c), wf_rows(n, 1 - c), wf_send.at[n], wf_recv.at[n], mate)

    def wo_first():
        for dy in (1, 3):
            wy_arrival(dy).wait_recv()
            wr_copy(0 if dy == 1 else 1).start()
            for n in range(4):
                wn_copy(4 - dy, n).start()
            wf_copy(2 if dy == 1 else 1).start()

    def wo_second():
        for r in range(2):
            wr_arrival(r).wait_recv()
            wn_copy(2, 2 * r).start()
            wn_copy(2, 2 * r + 1).start()
            wf_copy(3 + r).start()
        for b in (3, 1):
            for n in range(4):
                wn_arrival(b, n).wait_recv()
            wf_copy(4 + b).start()

    def wo_third():
        for n in range(4):
            wn_arrival(2, n).wait_recv()
        wf_copy(6).start()
        for n in range(8):
            wf_arrival(n).wait_recv()

    for dy in (1, 3):
        wy_copy(dy).start()

    owner_q = s // 2
    block = s % 2

    def sb_src(h, who):
        return st.at[pl.ds(aligned(half * h + part * block + (who // 4) * 16, 8), 16),
                     pl.ds(aligned((who % 4) * lane4, 128), lane4)]

    def sb_copy(k, h):
        return remote(sb_src(h, seq_peer(k)), stb.at[h], sb_send.at[h, k - 1], sb_recv.at[h], (s, seq_peer(k)))

    @pl.when(q == owner_q)
    def _():
        for h in range(2):
            each(1, SEQ_DEVS, lambda k: sb_copy(k, h).start())
            stb[h] = sb_src(h, q)[...]

    for n in range(3):
        w2_copy(n).start()

    each(1, STEP_DEVS, lambda k: te_arrival(k).wait_recv())
    for n in range(STEP_DEVS):
        tes[2 * n:2 * n + 2, :] = tea[n]
    own = st[...]
    transposed = (((1,), (1,)), ((), ()))

    def parts(values):
        high = values.astype(BF16)
        return high, (values - high.astype(F32)).astype(BF16)

    def dot_t(a, b):
        return lax.dot_general(a, b, transposed, preferred_element_type=F32)

    own_parts, te_parts, square_parts = parts(own), parts(tes[...]), parts(own * own)
    cross = dot_t(te_parts[0], own_parts[0]) + dot_t(te_parts[1], own_parts[0]) + dot_t(te_parts[0], own_parts[1])
    one_row = jnp.ones((16, width), BF16)
    squares = (dot_t(one_row, square_parts[0]) + dot_t(one_row, square_parts[1]))[0:1]
    step_squares = jnp.sum(tes[...] * tes[...], axis=1, keepdims=True)
    mean_square = jnp.maximum((squares + 2.0 * cross + step_squares) * (1.0 / width), 0.0)
    rtb[q] = lax.rsqrt(mean_square + NORM_EPS)

    def rt_copy(k):
        return remote(rtb.at[q], rtb.at[q], rt_send.at[k - 1], rt_recv.at[k - 1], (s, seq_peer(k)))

    def rt_arrival(k):
        return remote(rtb.at[q], rtb.at[seq_peer(SEQ_DEVS - k)], rt_send.at[k - 1], rt_recv.at[k - 1], here)

    each(1, SEQ_DEVS, lambda k: rt_copy(k).start())
    tew[...] = split_dot(tes[...], w1[...]) * factor

    for dy in (1, 3, 2):
        sw_arrival(dy).wait_recv()
        sw_forward(dy).start()
    each(1, SEQ_DEVS, lambda k: rt_arrival(k).wait_recv())
    for dy in range(4):
        sw_forwarded(dy).wait_recv()

    pick_row = lax.broadcasted_iota(jnp.int32, (STEPS, 4 * HEAD_SIZE), 0)
    pick_lane = lax.broadcasted_iota(jnp.int32, (STEPS, 4 * HEAD_SIZE), 1)
    pick = (pick_row == 4 * q + pick_lane // HEAD_SIZE).astype(BF16)

    def build(b):
        scales = sum(lax.dot_general(rows, pick, (((0,), (0,)), ((), ())), preferred_element_type=F32)
                     for rows in parts(rtb[b]))
        base = swb[b].astype(F32)
        for i in range(4):
            rows = scales[:, i * HEAD_SIZE:(i + 1) * HEAD_SIZE]
            step_row = tew[pl.ds(4 * q + i, 1), :]
            for n3 in range(3):
                cols = slice(n3 * HEAD_SIZE, (n3 + 1) * HEAD_SIZE)
                qkv1[i, b, :, cols] = ((base[:, cols] + step_row[:, cols]) * rows).astype(BF16)

    each(0, SEQ_DEVS, build)

    def a1_copy(h, k):
        return remote(att1.at[h, step_peer(k)], recv1.at[h, :, pl.ds(aligned(s * HEAD_SIZE, 128), HEAD_SIZE)],
                      a1_send.at[h, k - 1], a1_recv.at[h, k - 1], (step_peer(k), q))

    def a1_arrival(h, k):
        src = step_peer(STEP_DEVS - k)
        return remote(att1.at[h, s], recv1.at[h, :, pl.ds(aligned(src * HEAD_SIZE, 128), HEAD_SIZE)],
                      a1_send.at[h, k - 1], a1_recv.at[h, k - 1], here)

    for h in range(2):
        def attend1(i):
            keys = qkv1[i, :, :, HEAD_SIZE:2 * HEAD_SIZE].reshape(8 * tok, HEAD_SIZE)
            values = qkv1[i, :, :, 2 * HEAD_SIZE:3 * HEAD_SIZE].reshape(8 * tok, HEAD_SIZE)
            mixed = [softmax_mix(qkv1[i, 4 * sub:4 * sub + 4, half * h:half * (h + 1), 0:HEAD_SIZE].reshape(
                4 * half, HEAD_SIZE), keys, values) for sub in range(2)]
            for sub in range(2):
                att1[h, 8 * sub:8 * sub + 8, pl.ds(aligned(i * part, part), part), :] = mixed[sub].reshape(
                    8, part, HEAD_SIZE)

        each(0, 4, attend1)
        each(1, STEP_DEVS, lambda k: a1_copy(h, k).start())
        recv1[h, :, pl.ds(aligned(s * HEAD_SIZE, 128), HEAD_SIZE)] = att1[h, s]
        if h == 0:
            wo_own.wait()
            wf_copy(0).start()
            wo_first()
        else:
            wo_second()

    def piece(ref, who):
        return ref.at[pl.ds(aligned((who // 4) * 16, 16), 16), pl.ds(aligned((who % 4) * lane4, 128), lane4)]

    def p1_copy(h, k):
        dest = seq_peer(k)
        return remote(piece(bs1.at[h], dest), pr1.at[h, q], p1_send.at[h, k - 1], p1_recv.at[h, k - 1], (s, dest))

    def p1_arrival(h, k):
        return remote(piece(bs1.at[h], q), pr1.at[h, seq_peer(SEQ_DEVS - k)],
                      p1_send.at[h, k - 1], p1_recv.at[h, k - 1], here)

    def e1_copy(h, k):
        dest = seq_peer(k)
        return remote(pe1.at[h, dest], piece(e1.at[h], q), e1_send.at[h, k - 1], e1_recv.at[h, k - 1], (s, dest))

    def e1_arrival(h, k):
        return remote(pe1.at[h, q], piece(e1.at[h], seq_peer(SEQ_DEVS - k)),
                      e1_send.at[h, k - 1], e1_recv.at[h, k - 1], here)

    def drift1(h):
        each(1, STEP_DEVS, lambda k: a1_arrival(h, k).wait_recv())

        def tile(n):
            cols = pl.ds(aligned(n * 256, 256), 256)
            rows = jnp.dot(recv1[h], wo[:, cols], preferred_element_type=F32)
            total = rows[0:part]
            dr1[h, 0, :, cols] = total
            for i in range(1, 4):
                total = total + rows[i * part:(i + 1) * part]
                dr1[h, i, :, cols] = total
            bs1[h, :, cols] = total.astype(BF16)

        each(0, width // 256, tile)
        each(1, SEQ_DEVS, lambda k: p1_copy(h, k).start())
        pr1[h, q] = piece(bs1.at[h], q)[...]

    def scan1(h):
        each(1, SEQ_DEVS, lambda k: p1_arrival(h, k).wait_recv())
        total = jnp.zeros((16, lane4), F32)
        for k in range(SEQ_DEVS):
            pe1[h, k] = stb[h] + scale * total
            total = total + pr1[h, k].astype(F32)
        each(1, SEQ_DEVS, lambda k: e1_copy(h, k).start())
        piece(e1.at[h], q)[...] = pe1[h, q]

    def x_rows(h, who):
        return xs.at[pl.ds(aligned(h * 8 * half + who * part, part), part)]

    def x_target(h, n):
        i, e = n // 2, n % 2
        return 2 * q + i // 2, 2 * (2 * (i % 2) + e) + lax.rem(s + h, 2)

    def x_copy(h, n):
        return remote(ns.at[h, n // 2], x_rows(h, s), x_send.at[h, n], x_recv.at[h, s // 2], x_target(h, n))

    def is_here(h, n):
        a, b = x_target(h, n)
        return jnp.logical_and(a == s, b == q)

    def x_local(h, n):
        return pltpu.make_async_copy(ns.at[h, n // 2], x_rows(h, s), x_recv.at[h, s // 2])

    def direct(h, m):
        return 2 * m + lax.rem(c + h, 2)

    def x_arrival(h, m):
        rows = x_rows(h, direct(h, m))
        return pltpu.make_async_copy(rows, rows, x_recv.at[h, m])

    def x_forward(h, m):
        rows = x_rows(h, direct(h, m))
        return remote(rows, rows, xf_send.at[h, m], xf_recv.at[h, m], mate)

    def x_forwarded(h, m):
        rows = x_rows(h, 2 * m + lax.rem(c + h + 1, 2))
        return remote(rows, rows, xf_send.at[h, m], xf_recv.at[h, m], mate)

    def states(h):
        each(1, SEQ_DEVS, lambda k: e1_arrival(h, k).wait_recv())
        for i in range(4):
            shifted = e1[h] + tes[pl.ds(4 * q + i, 1), :]
            if i:
                shifted = shifted + scale * dr1[h, i - 1]
            mean = jnp.mean(shifted * shifted, axis=1, keepdims=True)
            ns[h, i] = (shifted * lax.rsqrt(mean + NORM_EPS)).astype(BF16)
            for n in (2 * i, 2 * i + 1):
                @pl.when(is_here(h, n))
                def _():
                    x_local(h, n).start()

                @pl.when(jnp.logical_not(is_here(h, n)))
                def _():
                    x_copy(h, n).start()

    @pl.when(q != owner_q)
    def _():
        for h in range(2):
            sb_copy_in = remote(stb.at[h], stb.at[h], sb_send.at[h, 0], sb_recv.at[h], here)
            sb_copy_in.wait_recv()

    wo_third()
    drift1(0)
    scan1(0)
    drift1(1)
    states(0)
    scan1(1)
    states(1)

    for n in range(3):
        w2_copy(n).wait()

    def project(h, sub):
        rows = pl.ds(h * 8 * half + sub * 4 * half, 4 * half)

        def columns(n):
            cols = pl.ds(aligned(n * gw, gw), gw)
            f = jnp.where(n == 0, QUERY_SCALE, 1.0)
            qkv2[rows, cols] = (jnp.dot(xs[rows, :], w2[:, cols], preferred_element_type=F32) * f).astype(BF16)

        each(0, 3, columns)

    for h in range(2):
        for sub in range(2):
            for m in range(4 * sub, 4 * sub + 4):
                x_arrival(h, m).wait()
                x_forward(h, m).start()
        for sub in range(2):
            for m in range(4 * sub, 4 * sub + 4):
                x_forwarded(h, m).wait_recv()
            project(h, sub)

    def a2_block(h, who):
        yy, cc = who // 2, who % 2
        return recv2.at[h, pl.ds(aligned((yy // 2) * half, half), half),
                        pl.ds(aligned(((yy % 2) * 2 + cc) * gw, gw), gw)]

    def att2_rows(h, who):
        return att2.at[pl.ds(aligned(h * 8 * half + who * half, half), half)]

    def a2_copy(h, k):
        dest = seq_peer(k)
        return remote(att2_rows(h, dest), a2_block(h, q), a2_send.at[h, k - 1], a2_recv.at[h, k - 1], (s, dest))

    def a2_arrival(h, k):
        return remote(att2_rows(h, q), a2_block(h, seq_peer(SEQ_DEVS - k)),
                      a2_send.at[h, k - 1], a2_recv.at[h, k - 1], here)

    def a2_own(h):
        return pltpu.make_async_copy(att2_rows(h, q), a2_block(h, q), a2_sem.at[h])

    for h in range(2):
        def attend2(head):
            def cols(p):
                return pl.ds(aligned(p * gw + head * HEAD_SIZE, HEAD_SIZE), HEAD_SIZE)

            rows = [pl.ds(h * 8 * half + sub * 4 * half, 4 * half) for sub in range(2)]
            mixed = [softmax_mix(qkv2[r, cols(0)], qkv2[:, cols(1)], qkv2[:, cols(2)]) for r in rows]
            for r, m in zip(rows, mixed):
                att2[r, cols(0)] = m

        each(0, 4, attend2)
        each(1, SEQ_DEVS, lambda k: a2_copy(h, k).start())
        a2_own(h).start()

    def p2_copy(h, k):
        dest = step_peer(k)
        return remote(piece(bs2.at[h], dest), pr2.at[h, s], p2_send.at[h, k - 1], p2_recv.at[h, k - 1], (dest, q))

    def p2_arrival(h, k):
        return remote(piece(bs2.at[h], s), pr2.at[h, step_peer(STEP_DEVS - k)],
                      p2_send.at[h, k - 1], p2_recv.at[h, k - 1], here)

    def e2_copy(h, k):
        dest = step_peer(k)
        return remote(pe2.at[h, dest], piece(e2.at[h], s), e2_send.at[h, k - 1], e2_recv.at[h, k - 1], (dest, q))

    def e2_arrival(h, k):
        return remote(pe2.at[h, s], piece(e2.at[h], step_peer(STEP_DEVS - k)),
                      e2_send.at[h, k - 1], e2_recv.at[h, k - 1], here)

    def drift2(h):
        a2_own(h).wait()
        each(1, SEQ_DEVS, lambda k: a2_arrival(h, k).wait_recv())

        def tile(n):
            cols = pl.ds(aligned(n * 256, 256), 256)
            rows = jnp.dot(recv2[h], wo[:, cols], preferred_element_type=F32)
            first = rows[0:half]
            total = first + rows[half:]
            dr2[h, 0, :, cols] = first
            dr2[h, 1, :, cols] = total
            bs2[h, :, cols] = total.astype(BF16)

        each(0, width // 256, tile)
        each(1, STEP_DEVS, lambda k: p2_copy(h, k).start())
        pr2[h, s] = piece(bs2.at[h], s)[...]

    def scan2(h):
        each(1, STEP_DEVS, lambda k: p2_arrival(h, k).wait_recv())
        total = jnp.zeros((16, lane4), F32)
        for k in range(STEP_DEVS):
            pe2[h, k] = total
            total = total + pr2[h, k].astype(F32)
        each(1, STEP_DEVS, lambda k: e2_copy(h, k).start())
        piece(e2.at[h], s)[...] = pe2[h, s]

    def finish(h):
        each(1, STEP_DEVS, lambda k: e2_arrival(h, k).wait_recv())
        for i in range(2):
            for b in range(2):
                rows = slice(part * b, part * (b + 1))
                out_ref[i, half * b + part * h:half * b + part * (h + 1), :] = e2[h, rows, :] + dr2[h, i, rows, :]

    drift2(0)
    scan2(0)
    drift2(1)
    scan2(1)
    finish(0)
    finish(1)

    each(1, STEP_DEVS, lambda k: te_copy(k).wait_send())
    for dy in range(1, 4):
        sw_copy(dy).wait_send()
        for n in range(4):
            wn_copy(dy, n).wait_send()
    for dy in range(4):
        sw_forward(dy).wait_send()
    for n in range(8):
        wf_copy(n).wait_send()
    for r in range(2):
        wy_copy(1 + 2 * r).wait_send()
        wr_copy(r).wait_send()
    each(1, SEQ_DEVS, lambda k: rt_copy(k).wait_send())

    @pl.when(q == owner_q)
    def _():
        for h in range(2):
            each(1, SEQ_DEVS, lambda k: sb_copy(k, h).wait_send())

    for h in range(2):
        for k in range(1, SEQ_DEVS):
            p1_copy(h, k).wait_send()
            e1_copy(h, k).wait_send()
            a2_copy(h, k).wait_send()
        for k in range(1, STEP_DEVS):
            a1_copy(h, k).wait_send()
            p2_copy(h, k).wait_send()
            e2_copy(h, k).wait_send()
        for n in range(8):
            @pl.when(jnp.logical_not(is_here(h, n)))
            def _():
                x_copy(h, n).wait_send()
        for m in range(8):
            x_forward(h, m).wait_send()


def on_device(start_state, timesteps, qkv_weight, out_weight):
    tok, width = start_state.shape
    half, part, lane4 = tok // 2, tok // 4, width // 4
    te = embed(timesteps, width)
    dma = pltpu.SemaphoreType.DMA
    vmem = pl.BlockSpec(memory_space=pltpu.VMEM)
    hbm = pl.BlockSpec(memory_space=pl.ANY)
    sums = pl.pallas_call(
        kernel,
        out_shape=jax.ShapeDtypeStruct((2, tok, width), F32),
        in_specs=[vmem, hbm, hbm, hbm],
        out_specs=vmem,
        scratch_shapes=[
            pltpu.VMEM((width, 3 * HEAD_SIZE), BF16),
            pltpu.VMEM((width, 3 * INNER // 4), BF16),
            pltpu.VMEM((INNER, width), BF16),
            pltpu.VMEM((tok, width), F32),
            pltpu.VMEM((STEP_DEVS, 2, width), F32),
            pltpu.VMEM((STEPS, width), F32),
            pltpu.VMEM((SEQ_DEVS, tok, 3 * HEAD_SIZE), BF16),
            pltpu.VMEM((SEQ_DEVS, STEPS, tok), F32),
            pltpu.VMEM((STEPS, 3 * HEAD_SIZE), F32),
            pltpu.VMEM((4, SEQ_DEVS, tok, 3 * HEAD_SIZE), BF16),
            pltpu.VMEM((2, STEP_DEVS, 4 * part, HEAD_SIZE), BF16),
            pltpu.VMEM((2, 4 * part, INNER), BF16),
            pltpu.VMEM((2, 4, part, width), F32),
            pltpu.VMEM((2, part, width), BF16),
            pltpu.VMEM((2, SEQ_DEVS, 16, lane4), BF16),
            pltpu.VMEM((2, SEQ_DEVS, 16, lane4), F32),
            pltpu.VMEM((2, part, width), F32),
            pltpu.VMEM((2, 16, lane4), F32),
            pltpu.VMEM((2, 4, part, width), BF16),
            pltpu.VMEM((8 * tok, width), BF16),
            pltpu.VMEM((8 * tok, 3 * INNER // 4), BF16),
            pltpu.VMEM((8 * tok, INNER // 4), BF16),
            pltpu.VMEM((2, tok, INNER), BF16),
            pltpu.VMEM((2, 2, half, width), F32),
            pltpu.VMEM((2, half, width), BF16),
            pltpu.VMEM((2, STEP_DEVS, 16, lane4), BF16),
            pltpu.VMEM((2, STEP_DEVS, 16, lane4), F32),
            pltpu.VMEM((2, half, width), F32),
            dma((3,)), dma((3,)), dma, dma((4,)),
            dma((15,)), dma((15,)), dma((3,)), dma((3,)), dma((4,)), dma((4,)), dma((7,)), dma((7,)),
            dma((2, 7)), dma((2,)),
            dma((3,)), dma((3,)), dma((2,)), dma((2,)), dma((3, 4)), dma((3, 4)), dma((8,)), dma((8,)),
            dma((2, 15)), dma((2, 15)), dma((2, 7)), dma((2, 7)), dma((2, 7)), dma((2, 7)),
            dma((2, 8)), dma((2, 8)), dma((2, 8)), dma((2, 8)),
            dma((2, 7)), dma((2, 7)), dma((2,)), dma((2, 15)), dma((2, 15)), dma((2, 15)), dma((2, 15)),
        ],
        compiler_params=pltpu.CompilerParams(
            collective_id=0, has_side_effects=True, vmem_limit_bytes=58 * 1024 * 1024),
        name="picard",
    )(te, start_state, qkv_weight, out_weight)
    return start_state[None] + (1.0 / STEPS) * sums


def solution(mesh):
    return jax.shard_map(
        on_device,
        mesh=mesh,
        in_specs=(P("seq", None), P("step"), P(), P("seq", None)),
        out_specs=P("step", "seq", None),
        check_vma=False,
    )
```

```python
import functools
import math

import jax
import jax.numpy as jnp
from jax import lax
from jax.experimental import pallas as pl
from jax.experimental.pallas import tpu as pltpu
from jax.sharding import PartitionSpec as P

HEAD_SIZE = 128
HEADS = 16
INNER = HEADS * HEAD_SIZE
STEP_DEVS = 16
SEQ_DEVS = 8
STEPS = 32
NORM_EPS = 1e-06
MESH = pl.DeviceIdType.MESH
F32 = jnp.float32
BF16 = jnp.bfloat16
QUERY_SCALE = math.log2(math.e) / math.sqrt(HEAD_SIZE)


def embed(step_index, model_width):
    half_width = model_width // 2
    frequency = jnp.exp(-math.log(10000.0) * jnp.arange(half_width, dtype=F32) / half_width)
    angles = step_index.astype(F32)[:, None] * frequency[None, :]
    return jnp.concatenate([jnp.sin(angles), jnp.cos(angles)], axis=1)


def remote(src, dst, send_sem, recv_sem, device):
    return pltpu.make_async_remote_copy(
        src_ref=src, dst_ref=dst, send_sem=send_sem, recv_sem=recv_sem,
        device_id=device, device_id_type=MESH)


def aligned(value, by):
    return pl.multiple_of(value, by)


def each(first, last, body):
    def step(k, carry):
        body(k)
        return carry

    lax.fori_loop(first, last, step, 0)


def split_dot(values, weights):
    high = values.astype(BF16)
    low = (values - high.astype(F32)).astype(BF16)
    return (jnp.dot(high, weights, preferred_element_type=F32)
            + jnp.dot(low, weights, preferred_element_type=F32))


def score(queries, keys):
    return lax.dot_general(queries, keys, (((1,), (1,)), ((), ())), preferred_element_type=F32)


def mix(scores, values):
    expo = jnp.exp2(scores - jnp.max(scores, axis=1, keepdims=True))
    total = jnp.sum(expo, axis=1, keepdims=True)
    mixed = jnp.dot(expo.astype(BF16), values, preferred_element_type=F32)
    return (mixed / total).astype(BF16)


def kernel(
    te_ref, start_ref, wqkv_ref, wout_ref,
    out_ref,
    w1, w2, wo, st, tea, tes, swb, rtb, tew, qkv1, att1, recv1, dr1, bs1, pr1, pe1, e1, stb, ns,
    xs, qkv2, att2, recv2, dr2, bs2, pr2, pe2, e2, score_a, score_b,
    w1_sem, w2_sem, wo_sem, st_sem,
    te_send, te_recv, sw_send, sw_recv, swf_send, swf_recv, rt_send, rt_recv, sb_send, sb_recv,
    wy_send, wy_recv, wr_send, wr_recv, wn_send, wn_recv, wf_send, wf_recv,
    a1_send, a1_recv, p1_send, p1_recv, e1_send, e1_recv,
    x_send, x_recv, xf_send, xf_recv,
    a2_send, a2_recv, a2_sem, p2_send, p2_recv, e2_send, e2_recv,
):
    tok, width = start_ref.shape
    half, part = tok // 2, tok // 4
    lane4 = width // 4
    orow = wout_ref.shape[0]
    s = lax.axis_index("step")
    q = lax.axis_index("seq")
    y, c = q // 2, q % 2
    parity = y // 2
    group = (y % 2) * 2 + c
    gw = INNER // 4
    scale = 1.0 / STEPS
    here = (s, q)
    mate = (s, 2 * y + 1 - c)

    def chip(dy):
        return lax.rem(y + dy, 4)

    def step_peer(k):
        return lax.rem(s + k, STEP_DEVS)

    def seq_peer(k):
        return lax.rem(q + k, SEQ_DEVS)

    def w1_copy(n):
        return pltpu.make_async_copy(
            wqkv_ref.at[:, pl.ds(aligned(n * INNER + s * HEAD_SIZE, 128), HEAD_SIZE)],
            w1.at[:, pl.ds(n * HEAD_SIZE, HEAD_SIZE)], w1_sem.at[n])

    def w2_copy(n):
        return pltpu.make_async_copy(
            wqkv_ref.at[:, pl.ds(aligned(n * INNER + group * gw, 128), gw)],
            w2.at[:, pl.ds(n * gw, gw)], w2_sem.at[n])

    def st_copy(n):
        h, b = n // 2, n % 2
        return pltpu.make_async_copy(
            start_ref.at[pl.ds(half * b + part * h, part)],
            st.at[pl.ds(half * h + part * b, part)], st_sem.at[n])

    def wo_rows(owner, first, count):
        return wo.at[pl.ds(aligned(owner * orow + first, 16), count)]

    wo_own = pltpu.make_async_copy(wout_ref, wo_rows(q, 0, orow), wo_sem)
    for n in range(4):
        st_copy(n).start()
    for n in range(3):
        w1_copy(n).start()
    wo_own.start()

    barrier = pltpu.get_barrier_semaphore()
    each(1, STEP_DEVS, lambda k: pl.semaphore_signal(
        barrier, inc=1, device_id=(step_peer(k), q), device_id_type=MESH))
    each(1, SEQ_DEVS, lambda k: pl.semaphore_signal(
        barrier, inc=1, device_id=(s, seq_peer(k)), device_id_type=MESH))

    for n in range(4):
        st_copy(n).wait()
    for n in range(3):
        w1_copy(n).wait()
    lane = lax.broadcasted_iota(jnp.int32, (1, 3 * HEAD_SIZE), 1)
    factor = jnp.where(lane < HEAD_SIZE, QUERY_SCALE, 1.0)
    swb[q] = (split_dot(st[...], w1[...]) * factor).astype(BF16)
    pl.semaphore_wait(barrier, STEP_DEVS - 1 + SEQ_DEVS - 1)

    def te_copy(k):
        return remote(te_ref, tea.at[s], te_send.at[k - 1], te_recv.at[k - 1], (step_peer(k), q))

    def te_arrival(k):
        return remote(te_ref, tea.at[step_peer(STEP_DEVS - k)], te_send.at[k - 1], te_recv.at[k - 1], here)

    each(1, STEP_DEVS, lambda k: te_copy(k).start())
    tea[s] = te_ref[...]

    def sw_copy(dy):
        return remote(swb.at[q], swb.at[q], sw_send.at[dy - 1], sw_recv.at[dy - 1], (s, 2 * chip(dy) + c))

    def sw_arrival(dy):
        return remote(swb.at[q], swb.at[2 * chip(4 - dy) + c], sw_send.at[dy - 1], sw_recv.at[dy - 1], here)

    def sw_forward(dy):
        owner = 2 * chip(4 - dy) + c
        return remote(swb.at[owner], swb.at[owner], swf_send.at[dy % 4], swf_recv.at[dy % 4], mate)

    def sw_forwarded(dy):
        owner = 2 * chip(4 - dy) + 1 - c
        return remote(swb.at[owner], swb.at[owner], swf_send.at[dy % 4], swf_recv.at[dy % 4], mate)

    for dy in (2, 1, 3):
        sw_copy(dy).start()
    sw_forward(0).start()

    zx = (s // 4 + s) % 2
    hrow, qrow, erow = orow // 2, orow // 4, orow // 8

    def wo_of(n, core, first, count):
        return wo_rows(2 * chip(n) + core, first, count)

    def wy_copy(dy):
        return remote(wout_ref.at[pl.ds(aligned(zx * hrow, 16), hrow)], wo_rows(q, zx * hrow, hrow),
                      wy_send.at[dy - 1], wy_recv.at[dy - 1], (s, 2 * chip(dy) + c))

    def wy_arrival(dy):
        rows = wo_of(4 - dy, c, zx * hrow, hrow)
        return remote(rows, rows, wy_send.at[dy - 1], wy_recv.at[dy - 1], here)

    def wr_copy(r):
        rows = wo_of(1 if r else 3, c, zx * hrow + r * qrow, qrow)
        return remote(rows, rows, wr_send.at[r], wr_recv.at[r], (s, 2 * chip(3 if r else 1) + c))

    def wr_arrival(r):
        rows = wo_of(2, c, zx * hrow + r * qrow, qrow)
        return remote(rows, rows, wr_send.at[r], wr_recv.at[r], here)

    def neighbour(n):
        if n < 2:
            return step_peer(4 if n == 0 else STEP_DEVS - 4)
        return (s // 4) * 4 + lax.rem(s + (1 if n == 2 else 3), 4)

    def wn_copy(b, n):
        rows = wo_of(b, c, zx * hrow + n * erow, erow)
        return remote(rows, rows, wn_send.at[b - 1, n], wn_recv.at[b - 1, n], (neighbour(n), q))

    def wn_arrival(b, n):
        rows = wo_of(b, c, (1 - zx) * hrow + n * erow, erow)
        return remote(rows, rows, wn_send.at[b - 1, n], wn_recv.at[b - 1, n], here)

    def wf_rows(n, core):
        if n == 0:
            return wo_rows(2 * y + core, 0, orow)
        if n < 3:
            return wo_of(1 if n == 1 else 3, core, zx * hrow, hrow)
        if n < 5:
            return wo_of(2, core, zx * hrow + (n - 3) * qrow, qrow)
        return wo_of(n - 4, core, (1 - zx) * hrow, hrow)

    def wf_copy(n):
        return remote(wf_rows(n, c), wf_rows(n, c), wf_send.at[n], wf_recv.at[n], mate)

    def wf_arrival(n):
        return remote(wf_rows(n, 1 - c), wf_rows(n, 1 - c), wf_send.at[n], wf_recv.at[n], mate)

    def wo_first():
        for dy in (1, 3):
            wy_arrival(dy).wait_recv()
            wr_copy(0 if dy == 1 else 1).start()
            for n in range(4):
                wn_copy(4 - dy, n).start()
            wf_copy(2 if dy == 1 else 1).start()

    def wo_second():
        for r in range(2):
            wr_arrival(r).wait_recv()
            wn_copy(2, 2 * r).start()
            wn_copy(2, 2 * r + 1).start()
            wf_copy(3 + r).start()

    def wo_middle():
        for b in (3, 1):
            for n in range(4):
                wn_arrival(b, n).wait_recv()
            wf_copy(4 + b).start()

    def wo_third():
        for n in range(4):
            wn_arrival(2, n).wait_recv()
        wf_copy(6).start()
        for n in range(8):
            wf_arrival(n).wait_recv()


    owner_q = s // 2
    block = s % 2

    def sb_src(h, who):
        return st.at[pl.ds(aligned(half * h + part * block + (who // 4) * 16, 8), 16),
                     pl.ds(aligned((who % 4) * lane4, 128), lane4)]

    def sb_copy(k, h):
        return remote(sb_src(h, seq_peer(k)), stb.at[h], sb_send.at[h, k - 1], sb_recv.at[h], (s, seq_peer(k)))

    @pl.when(q == owner_q)
    def _():
        for h in range(2):
            each(1, SEQ_DEVS, lambda k: sb_copy(k, h).start())
            stb[h] = sb_src(h, q)[...]

    for n in range(3):
        w2_copy(n).start()

    each(1, STEP_DEVS, lambda k: te_arrival(k).wait_recv())
    for n in range(STEP_DEVS):
        tes[2 * n:2 * n + 2, :] = tea[n]
    own = st[...]
    transposed = (((1,), (1,)), ((), ()))

    def parts(values):
        high = values.astype(BF16)
        return high, (values - high.astype(F32)).astype(BF16)

    def dot_t(a, b):
        return lax.dot_general(a, b, transposed, preferred_element_type=F32)

    own_parts, te_parts, square_parts = parts(own), parts(tes[...]), parts(own * own)
    cross = dot_t(te_parts[0], own_parts[0]) + dot_t(te_parts[1], own_parts[0]) + dot_t(te_parts[0], own_parts[1])
    one_row = jnp.ones((16, width), BF16)
    squares = (dot_t(one_row, square_parts[0]) + dot_t(one_row, square_parts[1]))[0:1]
    step_squares = jnp.sum(tes[...] * tes[...], axis=1, keepdims=True)
    mean_square = jnp.maximum((squares + 2.0 * cross + step_squares) * (1.0 / width), 0.0)
    rtb[q] = lax.rsqrt(mean_square + NORM_EPS)

    def rt_copy(k):
        return remote(rtb.at[q], rtb.at[q], rt_send.at[k - 1], rt_recv.at[k - 1], (s, seq_peer(k)))

    def rt_arrival(k):
        return remote(rtb.at[q], rtb.at[seq_peer(SEQ_DEVS - k)], rt_send.at[k - 1], rt_recv.at[k - 1], here)

    each(1, SEQ_DEVS, lambda k: rt_copy(k).start())
    tew[...] = split_dot(tes[...], w1[...]) * factor

    for dy in (1, 3, 2):
        sw_arrival(dy).wait_recv()
        sw_forward(dy).start()
    each(1, SEQ_DEVS, lambda k: rt_arrival(k).wait_recv())
    for dy in range(4):
        sw_forwarded(dy).wait_recv()

    for dy in (1, 3):
        wy_copy(dy).start()

    pick_row = lax.broadcasted_iota(jnp.int32, (STEPS, 4 * HEAD_SIZE), 0)
    pick_lane = lax.broadcasted_iota(jnp.int32, (STEPS, 4 * HEAD_SIZE), 1)
    pick = (pick_row == 4 * q + pick_lane // HEAD_SIZE).astype(BF16)

    def build(b):
        scales = sum(lax.dot_general(rows, pick, (((0,), (0,)), ((), ())), preferred_element_type=F32)
                     for rows in parts(rtb[b]))
        base = swb[b].astype(F32)
        for i in range(4):
            rows = scales[:, i * HEAD_SIZE:(i + 1) * HEAD_SIZE]
            step_row = tew[pl.ds(4 * q + i, 1), :]
            for n3 in range(3):
                cols = slice(n3 * HEAD_SIZE, (n3 + 1) * HEAD_SIZE)
                qkv1[i, b, :, cols] = ((base[:, cols] + step_row[:, cols]) * rows).astype(BF16)

    each(0, SEQ_DEVS, build)

    def two_by_two(scores_of, mix_of):
        def pair(n):
            score_b[...] = scores_of(2 * n + 1)
            mix_of(2 * n, score_a[...])
            score_a[...] = scores_of(jnp.minimum(2 * n + 2, 3))
            mix_of(2 * n + 1, score_b[...])

        return pair

    def a1_copy(h, k):
        return remote(att1.at[h, step_peer(k)], recv1.at[h, :, pl.ds(aligned(s * HEAD_SIZE, 128), HEAD_SIZE)],
                      a1_send.at[h, k - 1], a1_recv.at[h, k - 1], (step_peer(k), q))

    def a1_arrival(h, k):
        src = step_peer(STEP_DEVS - k)
        return remote(att1.at[h, s], recv1.at[h, :, pl.ds(aligned(src * HEAD_SIZE, 128), HEAD_SIZE)],
                      a1_send.at[h, k - 1], a1_recv.at[h, k - 1], here)

    for h in range(2):
        def scores1(i):
            queries = qkv1[i, :, half * h:half * (h + 1), 0:HEAD_SIZE].reshape(8 * half, HEAD_SIZE)
            return score(queries, qkv1[i, :, :, HEAD_SIZE:2 * HEAD_SIZE].reshape(8 * tok, HEAD_SIZE))

        def mix1(i, scores):
            values = qkv1[i, :, :, 2 * HEAD_SIZE:3 * HEAD_SIZE].reshape(8 * tok, HEAD_SIZE)
            att1[h, :, pl.ds(aligned(i * part, part), part), :] = mix(scores, values).reshape(
                STEP_DEVS, part, HEAD_SIZE)

        attend1 = two_by_two(scores1, mix1)
        score_a[...] = scores1(0)
        if h == 0:
            wo_own.wait()
            wf_copy(0).start()
            each(0, 1, attend1)
            wo_first()
            each(1, 2, attend1)
        else:
            each(0, 1, attend1)
            wo_second()
            each(1, 2, attend1)
        each(1, STEP_DEVS, lambda k: a1_copy(h, k).start())
        recv1[h, :, pl.ds(aligned(s * HEAD_SIZE, 128), HEAD_SIZE)] = att1[h, s]

    wo_middle()

    def piece(ref, who):
        return ref.at[pl.ds(aligned((who // 4) * 16, 16), 16), pl.ds(aligned((who % 4) * lane4, 128), lane4)]

    def p1_copy(h, k):
        dest = seq_peer(k)
        return remote(piece(bs1.at[h], dest), pr1.at[h, q], p1_send.at[h, k - 1], p1_recv.at[h, k - 1], (s, dest))

    def p1_arrival(h, k):
        return remote(piece(bs1.at[h], q), pr1.at[h, seq_peer(SEQ_DEVS - k)],
                      p1_send.at[h, k - 1], p1_recv.at[h, k - 1], here)

    def e1_copy(h, k):
        dest = seq_peer(k)
        return remote(pe1.at[h, dest], piece(e1.at[h], q), e1_send.at[h, k - 1], e1_recv.at[h, k - 1], (s, dest))

    def e1_arrival(h, k):
        return remote(pe1.at[h, q], piece(e1.at[h], seq_peer(SEQ_DEVS - k)),
                      e1_send.at[h, k - 1], e1_recv.at[h, k - 1], here)

    def drift1(h):
        each(1, STEP_DEVS, lambda k: a1_arrival(h, k).wait_recv())

        def tile(n):
            cols = pl.ds(aligned(n * 256, 256), 256)
            rows = jnp.dot(recv1[h], wo[:, cols], preferred_element_type=F32)
            total = rows[0:part]
            dr1[h, 0, :, cols] = total
            for i in range(1, 4):
                total = total + rows[i * part:(i + 1) * part]
                dr1[h, i, :, cols] = total
            bs1[h, :, cols] = total.astype(BF16)

        each(0, width // 256, tile)
        each(1, SEQ_DEVS, lambda k: p1_copy(h, k).start())
        pr1[h, q] = piece(bs1.at[h], q)[...]

    def scan1(h):
        each(1, SEQ_DEVS, lambda k: p1_arrival(h, k).wait_recv())
        total = jnp.zeros((16, lane4), F32)
        for k in range(SEQ_DEVS):
            pe1[h, k] = stb[h] + scale * total
            total = total + pr1[h, k].astype(F32)
        each(1, SEQ_DEVS, lambda k: e1_copy(h, k).start())
        piece(e1.at[h], q)[...] = pe1[h, q]

    def x_rows(h, who):
        return xs.at[pl.ds(aligned(h * 8 * half + who * part, part), part)]

    def x_target(h, n):
        i, e = n // 2, n % 2
        return 2 * q + i // 2, 2 * (2 * (i % 2) + e) + lax.rem(s + h, 2)

    def x_copy(h, n):
        return remote(ns.at[h, n // 2], x_rows(h, s), x_send.at[h, n], x_recv.at[h, s // 2], x_target(h, n))

    def is_here(h, n):
        a, b = x_target(h, n)
        return jnp.logical_and(a == s, b == q)

    def x_local(h, n):
        return pltpu.make_async_copy(ns.at[h, n // 2], x_rows(h, s), x_recv.at[h, s // 2])

    def direct(h, m):
        return 2 * m + lax.rem(c + h, 2)

    def x_arrival(h, m):
        rows = x_rows(h, direct(h, m))
        return pltpu.make_async_copy(rows, rows, x_recv.at[h, m])

    def x_forward(h, m):
        rows = x_rows(h, direct(h, m))
        return remote(rows, rows, xf_send.at[h, m], xf_recv.at[h, m], mate)

    def x_forwarded(h, m):
        rows = x_rows(h, 2 * m + lax.rem(c + h + 1, 2))
        return remote(rows, rows, xf_send.at[h, m], xf_recv.at[h, m], mate)

    def states(h):
        each(1, SEQ_DEVS, lambda k: e1_arrival(h, k).wait_recv())
        for i in range(4):
            shifted = e1[h] + tes[pl.ds(4 * q + i, 1), :]
            if i:
                shifted = shifted + scale * dr1[h, i - 1]
            mean = jnp.mean(shifted * shifted, axis=1, keepdims=True)
            ns[h, i] = (shifted * lax.rsqrt(mean + NORM_EPS)).astype(BF16)
            for n in (2 * i, 2 * i + 1):
                @pl.when(is_here(h, n))
                def _():
                    x_local(h, n).start()

                @pl.when(jnp.logical_not(is_here(h, n)))
                def _():
                    x_copy(h, n).start()

    @pl.when(q != owner_q)
    def _():
        for h in range(2):
            sb_copy_in = remote(stb.at[h], stb.at[h], sb_send.at[h, 0], sb_recv.at[h], here)
            sb_copy_in.wait_recv()

    wo_third()
    drift1(0)
    scan1(0)
    drift1(1)
    states(0)
    scan1(1)
    states(1)

    for n in range(3):
        w2_copy(n).wait()

    def project(h, sub):
        rows = pl.ds(h * 8 * half + sub * 4 * half, 4 * half)

        def columns(n):
            cols = pl.ds(aligned(n * gw, gw), gw)
            f = jnp.where(n == 0, QUERY_SCALE, 1.0)
            qkv2[rows, cols] = (jnp.dot(xs[rows, :], w2[:, cols], preferred_element_type=F32) * f).astype(BF16)

        each(0, 3, columns)

    for h in range(2):
        for sub in range(2):
            for m in range(4 * sub, 4 * sub + 4):
                x_arrival(h, m).wait()
                x_forward(h, m).start()
        for sub in range(2):
            for m in range(4 * sub, 4 * sub + 4):
                x_forwarded(h, m).wait_recv()
            project(h, sub)

    def a2_block(h, who):
        yy, cc = who // 2, who % 2
        return recv2.at[h, pl.ds(aligned((yy // 2) * half, half), half),
                        pl.ds(aligned(((yy % 2) * 2 + cc) * gw, gw), gw)]

    def att2_rows(h, who):
        return att2.at[pl.ds(aligned(h * 8 * half + who * half, half), half)]

    def a2_copy(h, k):
        dest = seq_peer(k)
        return remote(att2_rows(h, dest), a2_block(h, q), a2_send.at[h, k - 1], a2_recv.at[h, k - 1], (s, dest))

    def a2_arrival(h, k):
        return remote(att2_rows(h, q), a2_block(h, seq_peer(SEQ_DEVS - k)),
                      a2_send.at[h, k - 1], a2_recv.at[h, k - 1], here)

    def a2_own(h):
        return pltpu.make_async_copy(att2_rows(h, q), a2_block(h, q), a2_sem.at[h])

    for h in range(2):
        rows = pl.ds(h * 8 * half, 8 * half)

        def cols(p, head):
            return pl.ds(aligned(p * gw + head * HEAD_SIZE, HEAD_SIZE), HEAD_SIZE)

        def scores2(head):
            return score(qkv2[rows, cols(0, head)], qkv2[:, cols(1, head)])

        def mix2(head, scores):
            att2[rows, cols(0, head)] = mix(scores, qkv2[:, cols(2, head)])

        score_a[...] = scores2(0)
        each(0, 2, two_by_two(scores2, mix2))
        each(1, SEQ_DEVS, lambda k: a2_copy(h, k).start())
        a2_own(h).start()

    def p2_copy(h, k):
        dest = step_peer(k)
        return remote(piece(bs2.at[h], dest), pr2.at[h, s], p2_send.at[h, k - 1], p2_recv.at[h, k - 1], (dest, q))

    def p2_arrival(h, k):
        return remote(piece(bs2.at[h], s), pr2.at[h, step_peer(STEP_DEVS - k)],
                      p2_send.at[h, k - 1], p2_recv.at[h, k - 1], here)

    def e2_copy(h, k):
        dest = step_peer(k)
        return remote(pe2.at[h, dest], piece(e2.at[h], s), e2_send.at[h, k - 1], e2_recv.at[h, k - 1], (dest, q))

    def e2_arrival(h, k):
        return remote(pe2.at[h, s], piece(e2.at[h], step_peer(STEP_DEVS - k)),
                      e2_send.at[h, k - 1], e2_recv.at[h, k - 1], here)

    def drift2(h):
        a2_own(h).wait()
        each(1, SEQ_DEVS, lambda k: a2_arrival(h, k).wait_recv())

        def tile(n):
            cols = pl.ds(aligned(n * 256, 256), 256)
            rows = jnp.dot(recv2[h], wo[:, cols], preferred_element_type=F32)
            first = rows[0:half]
            total = first + rows[half:]
            dr2[h, 0, :, cols] = first
            dr2[h, 1, :, cols] = total
            bs2[h, :, cols] = total.astype(BF16)

        each(0, width // 256, tile)
        each(1, STEP_DEVS, lambda k: p2_copy(h, k).start())
        pr2[h, s] = piece(bs2.at[h], s)[...]

    def scan2(h):
        each(1, STEP_DEVS, lambda k: p2_arrival(h, k).wait_recv())
        total = jnp.zeros((16, lane4), F32)
        for k in range(STEP_DEVS):
            pe2[h, k] = total
            total = total + pr2[h, k].astype(F32)
        each(1, STEP_DEVS, lambda k: e2_copy(h, k).start())
        piece(e2.at[h], s)[...] = pe2[h, s]

    def finish(h):
        each(1, STEP_DEVS, lambda k: e2_arrival(h, k).wait_recv())
        for i in range(2):
            for b in range(2):
                rows = slice(part * b, part * (b + 1))
                out_ref[i, half * b + part * h:half * b + part * (h + 1), :] = e2[h, rows, :] + dr2[h, i, rows, :]

    drift2(0)
    scan2(0)
    drift2(1)
    scan2(1)
    finish(0)
    finish(1)

    each(1, STEP_DEVS, lambda k: te_copy(k).wait_send())
    for dy in range(1, 4):
        sw_copy(dy).wait_send()
        for n in range(4):
            wn_copy(dy, n).wait_send()
    for dy in range(4):
        sw_forward(dy).wait_send()
    for n in range(8):
        wf_copy(n).wait_send()
    for r in range(2):
        wy_copy(1 + 2 * r).wait_send()
        wr_copy(r).wait_send()
    each(1, SEQ_DEVS, lambda k: rt_copy(k).wait_send())

    @pl.when(q == owner_q)
    def _():
        for h in range(2):
            each(1, SEQ_DEVS, lambda k: sb_copy(k, h).wait_send())

    for h in range(2):
        for k in range(1, SEQ_DEVS):
            p1_copy(h, k).wait_send()
            e1_copy(h, k).wait_send()
            a2_copy(h, k).wait_send()
        for k in range(1, STEP_DEVS):
            a1_copy(h, k).wait_send()
            p2_copy(h, k).wait_send()
            e2_copy(h, k).wait_send()
        for n in range(8):
            @pl.when(jnp.logical_not(is_here(h, n)))
            def _():
                x_copy(h, n).wait_send()
        for m in range(8):
            x_forward(h, m).wait_send()


def on_device(start_state, timesteps, qkv_weight, out_weight):
    tok, width = start_state.shape
    half, part, lane4 = tok // 2, tok // 4, width // 4
    te = embed(timesteps, width)
    dma = pltpu.SemaphoreType.DMA
    vmem = pl.BlockSpec(memory_space=pltpu.VMEM)
    hbm = pl.BlockSpec(memory_space=pl.ANY)
    sums = pl.pallas_call(
        kernel,
        out_shape=jax.ShapeDtypeStruct((2, tok, width), F32),
        in_specs=[vmem, hbm, hbm, hbm],
        out_specs=vmem,
        scratch_shapes=[
            pltpu.VMEM((width, 3 * HEAD_SIZE), BF16),
            pltpu.VMEM((width, 3 * INNER // 4), BF16),
            pltpu.VMEM((INNER, width), BF16),
            pltpu.VMEM((tok, width), F32),
            pltpu.VMEM((STEP_DEVS, 2, width), F32),
            pltpu.VMEM((STEPS, width), F32),
            pltpu.VMEM((SEQ_DEVS, tok, 3 * HEAD_SIZE), BF16),
            pltpu.VMEM((SEQ_DEVS, STEPS, tok), F32),
            pltpu.VMEM((STEPS, 3 * HEAD_SIZE), F32),
            pltpu.VMEM((4, SEQ_DEVS, tok, 3 * HEAD_SIZE), BF16),
            pltpu.VMEM((2, STEP_DEVS, 4 * part, HEAD_SIZE), BF16),
            pltpu.VMEM((2, 4 * part, INNER), BF16),
            pltpu.VMEM((2, 4, part, width), F32),
            pltpu.VMEM((2, part, width), BF16),
            pltpu.VMEM((2, SEQ_DEVS, 16, lane4), BF16),
            pltpu.VMEM((2, SEQ_DEVS, 16, lane4), F32),
            pltpu.VMEM((2, part, width), F32),
            pltpu.VMEM((2, 16, lane4), F32),
            pltpu.VMEM((2, 4, part, width), BF16),
            pltpu.VMEM((8 * tok, width), BF16),
            pltpu.VMEM((8 * tok, 3 * INNER // 4), BF16),
            pltpu.VMEM((8 * tok, INNER // 4), BF16),
            pltpu.VMEM((2, tok, INNER), BF16),
            pltpu.VMEM((2, 2, half, width), F32),
            pltpu.VMEM((2, half, width), BF16),
            pltpu.VMEM((2, STEP_DEVS, 16, lane4), BF16),
            pltpu.VMEM((2, STEP_DEVS, 16, lane4), F32),
            pltpu.VMEM((2, half, width), F32),
            pltpu.VMEM((8 * half, 8 * tok), F32),
            pltpu.VMEM((8 * half, 8 * tok), F32),
            dma((3,)), dma((3,)), dma, dma((4,)),
            dma((15,)), dma((15,)), dma((3,)), dma((3,)), dma((4,)), dma((4,)), dma((7,)), dma((7,)),
            dma((2, 7)), dma((2,)),
            dma((3,)), dma((3,)), dma((2,)), dma((2,)), dma((3, 4)), dma((3, 4)), dma((8,)), dma((8,)),
            dma((2, 15)), dma((2, 15)), dma((2, 7)), dma((2, 7)), dma((2, 7)), dma((2, 7)),
            dma((2, 8)), dma((2, 8)), dma((2, 8)), dma((2, 8)),
            dma((2, 7)), dma((2, 7)), dma((2,)), dma((2, 15)), dma((2, 15)), dma((2, 15)), dma((2, 15)),
        ],
        compiler_params=pltpu.CompilerParams(
            collective_id=0, has_side_effects=True, vmem_limit_bytes=58 * 1024 * 1024),
        name="picard",
    )(te, start_state, qkv_weight, out_weight)
    return start_state[None] + (1.0 / STEPS) * sums


def solution(mesh):
    return jax.shard_map(
        on_device,
        mesh=mesh,
        in_specs=(P("seq", None), P("step"), P(), P("seq", None)),
        out_specs=P("step", "seq", None),
        check_vma=False,
    )
```

```python
import functools
import math

import jax
import jax.numpy as jnp
from jax import lax
from jax.experimental import pallas as pl
from jax.experimental.pallas import tpu as pltpu
from jax.sharding import PartitionSpec as P

HEAD_SIZE = 128
HEADS = 16
INNER = HEADS * HEAD_SIZE
STEP_DEVS = 16
SEQ_DEVS = 8
STEPS = 32
NORM_EPS = 1e-06
MESH = pl.DeviceIdType.MESH
F32 = jnp.float32
BF16 = jnp.bfloat16
QUERY_SCALE = math.log2(math.e) / math.sqrt(HEAD_SIZE)


def embed(step_index, model_width):
    half_width = model_width // 2
    frequency = jnp.exp(-math.log(10000.0) * jnp.arange(half_width, dtype=F32) / half_width)
    angles = step_index.astype(F32)[:, None] * frequency[None, :]
    return jnp.concatenate([jnp.sin(angles), jnp.cos(angles)], axis=1)


def remote(src, dst, send_sem, recv_sem, device):
    return pltpu.make_async_remote_copy(
        src_ref=src, dst_ref=dst, send_sem=send_sem, recv_sem=recv_sem,
        device_id=device, device_id_type=MESH)


def aligned(value, by):
    return pl.multiple_of(value, by)


def each(first, last, body):
    def step(k, carry):
        body(k)
        return carry

    lax.fori_loop(first, last, step, 0)


def split_dot(values, weights):
    high = values.astype(BF16)
    low = (values - high.astype(F32)).astype(BF16)
    return (jnp.dot(high, weights, preferred_element_type=F32)
            + jnp.dot(low, weights, preferred_element_type=F32))


def score(queries, keys):
    return lax.dot_general(queries, keys, (((1,), (1,)), ((), ())), preferred_element_type=F32)


def mix(scores, values):
    expo = jnp.exp2(scores - jnp.max(scores, axis=1, keepdims=True))
    total = jnp.sum(expo, axis=1, keepdims=True)
    mixed = jnp.dot(expo.astype(BF16), values, preferred_element_type=F32)
    return (mixed / total).astype(BF16)


def kernel(
    te_ref, start_ref, wqkv_ref, wout_ref,
    out_ref,
    w1, w2, wo, st, tea, tes, swb, rtb, tew, qkv1, att1, recv1, dr1, bs1, pr1, pe1, e1, stb, ns,
    xs, qkv2, att2, recv2, dr2, bs2, pr2, pe2, e2, score_a, score_b,
    w1_sem, w2_sem, wo_sem, st_sem,
    te_send, te_recv, sw_send, sw_recv, swf_send, swf_recv, rt_send, rt_recv, sb_send, sb_recv,
    wy_send, wy_recv, wr_send, wr_recv, wn_send, wn_recv, wf_send, wf_recv,
    a1_send, a1_recv, p1_send, p1_recv, e1_send, e1_recv,
    x_send, x_recv, xf_send, xf_recv,
    a2_send, a2_recv, a2_sem, p2_send, p2_recv, e2_send, e2_recv,
):
    tok, width = start_ref.shape
    half, part = tok // 2, tok // 4
    lane4 = width // 4
    orow = wout_ref.shape[0]
    s = lax.axis_index("step")
    q = lax.axis_index("seq")
    y, c = q // 2, q % 2
    parity = y // 2
    group = (y % 2) * 2 + c
    gw = INNER // 4
    scale = 1.0 / STEPS
    here = (s, q)
    mate = (s, 2 * y + 1 - c)

    def chip(dy):
        return lax.rem(y + dy, 4)

    def step_peer(k):
        return lax.rem(s + k, STEP_DEVS)

    def seq_peer(k):
        return lax.rem(q + k, SEQ_DEVS)

    def w1_copy(n):
        return pltpu.make_async_copy(
            wqkv_ref.at[:, pl.ds(aligned(n * INNER + s * HEAD_SIZE, 128), HEAD_SIZE)],
            w1.at[:, pl.ds(n * HEAD_SIZE, HEAD_SIZE)], w1_sem.at[n])

    def w2_copy(n):
        return pltpu.make_async_copy(
            wqkv_ref.at[:, pl.ds(aligned(n * INNER + group * gw, 128), gw)],
            w2.at[:, pl.ds(n * gw, gw)], w2_sem.at[n])

    def st_copy(n):
        h, b = n // 2, n % 2
        return pltpu.make_async_copy(
            start_ref.at[pl.ds(half * b + part * h, part)],
            st.at[pl.ds(half * h + part * b, part)], st_sem.at[n])

    def wo_rows(owner, first, count):
        return wo.at[pl.ds(aligned(owner * orow + first, 16), count)]

    wo_own = pltpu.make_async_copy(wout_ref, wo_rows(q, 0, orow), wo_sem)
    for n in range(4):
        st_copy(n).start()
    for n in range(3):
        w1_copy(n).start()
    wo_own.start()

    barrier = pltpu.get_barrier_semaphore()
    each(1, STEP_DEVS, lambda k: pl.semaphore_signal(
        barrier, inc=1, device_id=(step_peer(k), q), device_id_type=MESH))
    each(1, SEQ_DEVS, lambda k: pl.semaphore_signal(
        barrier, inc=1, device_id=(s, seq_peer(k)), device_id_type=MESH))

    for n in range(4):
        st_copy(n).wait()
    for n in range(3):
        w1_copy(n).wait()
    lane = lax.broadcasted_iota(jnp.int32, (1, 3 * HEAD_SIZE), 1)
    factor = jnp.where(lane < HEAD_SIZE, QUERY_SCALE, 1.0)
    swb[q] = (split_dot(st[...], w1[...]) * factor).astype(BF16)
    pl.semaphore_wait(barrier, STEP_DEVS - 1 + SEQ_DEVS - 1)

    def te_copy(k):
        return remote(te_ref, tea.at[s], te_send.at[k - 1], te_recv.at[k - 1], (step_peer(k), q))

    def te_arrival(k):
        return remote(te_ref, tea.at[step_peer(STEP_DEVS - k)], te_send.at[k - 1], te_recv.at[k - 1], here)

    each(1, STEP_DEVS, lambda k: te_copy(k).start())
    tea[s] = te_ref[...]

    def sw_copy(dy):
        return remote(swb.at[q], swb.at[q], sw_send.at[dy - 1], sw_recv.at[dy - 1], (s, 2 * chip(dy) + c))

    def sw_arrival(dy):
        return remote(swb.at[q], swb.at[2 * chip(4 - dy) + c], sw_send.at[dy - 1], sw_recv.at[dy - 1], here)

    def sw_forward(dy):
        owner = 2 * chip(4 - dy) + c
        return remote(swb.at[owner], swb.at[owner], swf_send.at[dy % 4], swf_recv.at[dy % 4], mate)

    def sw_forwarded(dy):
        owner = 2 * chip(4 - dy) + 1 - c
        return remote(swb.at[owner], swb.at[owner], swf_send.at[dy % 4], swf_recv.at[dy % 4], mate)

    for dy in (2, 1, 3):
        sw_copy(dy).start()
    sw_forward(0).start()

    zx = (s // 4 + s) % 2
    hrow, qrow, erow = orow // 2, orow // 4, orow // 8

    def wo_of(n, core, first, count):
        return wo_rows(2 * chip(n) + core, first, count)

    def wy_copy(dy):
        return remote(wout_ref.at[pl.ds(aligned(zx * hrow, 16), hrow)], wo_rows(q, zx * hrow, hrow),
                      wy_send.at[dy - 1], wy_recv.at[dy - 1], (s, 2 * chip(dy) + c))

    def wy_arrival(dy):
        rows = wo_of(4 - dy, c, zx * hrow, hrow)
        return remote(rows, rows, wy_send.at[dy - 1], wy_recv.at[dy - 1], here)

    def wr_copy(r):
        rows = wo_of(1 if r else 3, c, zx * hrow + r * qrow, qrow)
        return remote(rows, rows, wr_send.at[r], wr_recv.at[r], (s, 2 * chip(3 if r else 1) + c))

    def wr_arrival(r):
        rows = wo_of(2, c, zx * hrow + r * qrow, qrow)
        return remote(rows, rows, wr_send.at[r], wr_recv.at[r], here)

    def neighbour(n):
        if n < 2:
            return step_peer(4 if n == 0 else STEP_DEVS - 4)
        return (s // 4) * 4 + lax.rem(s + (1 if n == 2 else 3), 4)

    def wn_copy(b, n):
        rows = wo_of(b, c, zx * hrow + n * erow, erow)
        return remote(rows, rows, wn_send.at[b - 1, n], wn_recv.at[b - 1, n], (neighbour(n), q))

    def wn_arrival(b, n):
        rows = wo_of(b, c, (1 - zx) * hrow + n * erow, erow)
        return remote(rows, rows, wn_send.at[b - 1, n], wn_recv.at[b - 1, n], here)

    def wf_rows(n, core):
        if n == 0:
            return wo_rows(2 * y + core, 0, orow)
        if n < 3:
            return wo_of(1 if n == 1 else 3, core, zx * hrow, hrow)
        if n < 5:
            return wo_of(2, core, zx * hrow + (n - 3) * qrow, qrow)
        return wo_of(n - 4, core, (1 - zx) * hrow, hrow)

    def wf_copy(n):
        return remote(wf_rows(n, c), wf_rows(n, c), wf_send.at[n], wf_recv.at[n], mate)

    def wf_arrival(n):
        return remote(wf_rows(n, 1 - c), wf_rows(n, 1 - c), wf_send.at[n], wf_recv.at[n], mate)

    def wo_first():
        for dy in (1, 3):
            wy_arrival(dy).wait_recv()
            wr_copy(0 if dy == 1 else 1).start()
            for n in range(4):
                wn_copy(4 - dy, n).start()
            wf_copy(2 if dy == 1 else 1).start()

    def wo_second():
        for r in range(2):
            wr_arrival(r).wait_recv()
            wn_copy(2, 2 * r).start()
            wn_copy(2, 2 * r + 1).start()
            wf_copy(3 + r).start()

    def wo_middle():
        for b in (3, 1):
            for n in range(4):
                wn_arrival(b, n).wait_recv()
            wf_copy(4 + b).start()

    def wo_third():
        for n in range(4):
            wn_arrival(2, n).wait_recv()
        wf_copy(6).start()
        for n in range(8):
            wf_arrival(n).wait_recv()


    owner_q = s // 2
    block = s % 2

    def sb_src(h, who):
        return st.at[pl.ds(aligned(half * h + part * block + (who // 4) * 16, 8), 16),
                     pl.ds(aligned((who % 4) * lane4, 128), lane4)]

    def sb_copy(k, h):
        return remote(sb_src(h, seq_peer(k)), stb.at[h], sb_send.at[h, k - 1], sb_recv.at[h], (s, seq_peer(k)))

    @pl.when(q == owner_q)
    def _():
        for h in range(2):
            each(1, SEQ_DEVS, lambda k: sb_copy(k, h).start())
            stb[h] = sb_src(h, q)[...]

    for n in range(3):
        w2_copy(n).start()

    each(1, STEP_DEVS, lambda k: te_arrival(k).wait_recv())
    for n in range(STEP_DEVS):
        tes[2 * n:2 * n + 2, :] = tea[n]
    own = st[...]
    transposed = (((1,), (1,)), ((), ()))

    def parts(values):
        high = values.astype(BF16)
        return high, (values - high.astype(F32)).astype(BF16)

    def dot_t(a, b):
        return lax.dot_general(a, b, transposed, preferred_element_type=F32)

    own_parts, te_parts, square_parts = parts(own), parts(tes[...]), parts(own * own)
    cross = dot_t(te_parts[0], own_parts[0]) + dot_t(te_parts[1], own_parts[0]) + dot_t(te_parts[0], own_parts[1])
    one_row = jnp.ones((16, width), BF16)
    squares = (dot_t(one_row, square_parts[0]) + dot_t(one_row, square_parts[1]))[0:1]
    step_squares = jnp.sum(tes[...] * tes[...], axis=1, keepdims=True)
    mean_square = jnp.maximum((squares + 2.0 * cross + step_squares) * (1.0 / width), 0.0)
    rtb[q] = lax.rsqrt(mean_square + NORM_EPS)

    def rt_copy(k):
        return remote(rtb.at[q], rtb.at[q], rt_send.at[k - 1], rt_recv.at[k - 1], (s, seq_peer(k)))

    def rt_arrival(k):
        return remote(rtb.at[q], rtb.at[seq_peer(SEQ_DEVS - k)], rt_send.at[k - 1], rt_recv.at[k - 1], here)

    each(1, SEQ_DEVS, lambda k: rt_copy(k).start())
    tew[...] = split_dot(tes[...], w1[...]) * factor

    for dy in (1, 3, 2):
        sw_arrival(dy).wait_recv()
        sw_forward(dy).start()
    each(1, SEQ_DEVS, lambda k: rt_arrival(k).wait_recv())
    for dy in range(4):
        sw_forwarded(dy).wait_recv()

    for dy in (1, 3):
        wy_copy(dy).start()

    pick_row = lax.broadcasted_iota(jnp.int32, (STEPS, 4 * HEAD_SIZE), 0)
    pick_lane = lax.broadcasted_iota(jnp.int32, (STEPS, 4 * HEAD_SIZE), 1)
    pick = (pick_row == 4 * q + pick_lane // HEAD_SIZE).astype(BF16)

    def build(b):
        scales = sum(lax.dot_general(rows, pick, (((0,), (0,)), ((), ())), preferred_element_type=F32)
                     for rows in parts(rtb[b]))
        base = swb[b].astype(F32)
        for i in range(4):
            rows = scales[:, i * HEAD_SIZE:(i + 1) * HEAD_SIZE]
            step_row = tew[pl.ds(4 * q + i, 1), :]
            for n3 in range(3):
                cols = slice(n3 * HEAD_SIZE, (n3 + 1) * HEAD_SIZE)
                qkv1[i, b, :, cols] = ((base[:, cols] + step_row[:, cols]) * rows).astype(BF16)

    each(0, SEQ_DEVS, build)

    def two_by_two(scores_of, mix_of):
        def pair(n):
            score_b[...] = scores_of(2 * n + 1)
            mix_of(2 * n, score_a[...])
            score_a[...] = scores_of(jnp.minimum(2 * n + 2, 3))
            mix_of(2 * n + 1, score_b[...])

        return pair

    def a1_copy(h, k):
        return remote(att1.at[h, step_peer(k)], recv1.at[h, :, pl.ds(aligned(s * HEAD_SIZE, 128), HEAD_SIZE)],
                      a1_send.at[h, k - 1], a1_recv.at[h, k - 1], (step_peer(k), q))

    def a1_arrival(h, k):
        src = step_peer(STEP_DEVS - k)
        return remote(att1.at[h, s], recv1.at[h, :, pl.ds(aligned(src * HEAD_SIZE, 128), HEAD_SIZE)],
                      a1_send.at[h, k - 1], a1_recv.at[h, k - 1], here)

    for h in range(2):
        def scores1(i):
            queries = qkv1[i, :, half * h:half * (h + 1), 0:HEAD_SIZE].reshape(8 * half, HEAD_SIZE)
            return score(queries, qkv1[i, :, :, HEAD_SIZE:2 * HEAD_SIZE].reshape(8 * tok, HEAD_SIZE))

        def mix1(i, scores):
            values = qkv1[i, :, :, 2 * HEAD_SIZE:3 * HEAD_SIZE].reshape(8 * tok, HEAD_SIZE)
            att1[h, :, pl.ds(aligned(i * part, part), part), :] = mix(scores, values).reshape(
                STEP_DEVS, part, HEAD_SIZE)

        attend1 = two_by_two(scores1, mix1)
        score_a[...] = scores1(0)
        if h == 0:
            wo_own.wait()
            wf_copy(0).start()
            each(0, 1, attend1)
            wo_first()
            each(1, 2, attend1)
        else:
            each(0, 1, attend1)
            wo_second()
            each(1, 2, attend1)
        each(1, STEP_DEVS, lambda k: a1_copy(h, k).start())
        recv1[h, :, pl.ds(aligned(s * HEAD_SIZE, 128), HEAD_SIZE)] = att1[h, s]

    wo_middle()

    def piece(ref, who):
        return ref.at[pl.ds(aligned((who // 4) * 16, 16), 16), pl.ds(aligned((who % 4) * lane4, 128), lane4)]

    def p1_copy(h, k):
        dest = seq_peer(k)
        return remote(piece(bs1.at[h], dest), pr1.at[h, q], p1_send.at[h, k - 1], p1_recv.at[h, k - 1], (s, dest))

    def p1_arrival(h, k):
        return remote(piece(bs1.at[h], q), pr1.at[h, seq_peer(SEQ_DEVS - k)],
                      p1_send.at[h, k - 1], p1_recv.at[h, k - 1], here)

    def e1_copy(h, k):
        dest = seq_peer(k)
        return remote(pe1.at[h, dest], piece(e1.at[h], q), e1_send.at[h, k - 1], e1_recv.at[h, k - 1], (s, dest))

    def e1_arrival(h, k):
        return remote(pe1.at[h, q], piece(e1.at[h], seq_peer(SEQ_DEVS - k)),
                      e1_send.at[h, k - 1], e1_recv.at[h, k - 1], here)

    def drift1(h):
        each(1, STEP_DEVS, lambda k: a1_arrival(h, k).wait_recv())

        def tile(n):
            cols = pl.ds(aligned(n * 256, 256), 256)
            rows = jnp.dot(recv1[h], wo[:, cols], preferred_element_type=F32)
            total = rows[0:part]
            dr1[h, 0, :, cols] = total
            for i in range(1, 4):
                total = total + rows[i * part:(i + 1) * part]
                dr1[h, i, :, cols] = total
            bs1[h, :, cols] = total.astype(BF16)

        each(0, width // 256, tile)
        each(1, SEQ_DEVS, lambda k: p1_copy(h, k).start())
        pr1[h, q] = piece(bs1.at[h], q)[...]

    def scan1(h):
        each(1, SEQ_DEVS, lambda k: p1_arrival(h, k).wait_recv())
        total = jnp.zeros((16, lane4), F32)
        for k in range(SEQ_DEVS):
            pe1[h, k] = stb[h] + scale * total
            total = total + pr1[h, k].astype(F32)
        each(1, SEQ_DEVS, lambda k: e1_copy(h, k).start())
        piece(e1.at[h], q)[...] = pe1[h, q]

    def x_rows(h, who):
        return xs.at[pl.ds(aligned(h * 8 * half + who * part, part), part)]

    def x_target(h, n):
        i, e = n // 2, n % 2
        return 2 * q + i // 2, 2 * (2 * (i % 2) + e) + lax.rem(s + h, 2)

    def x_copy(h, n):
        return remote(ns.at[h, n // 2], x_rows(h, s), x_send.at[h, n], x_recv.at[h, s // 2], x_target(h, n))

    def is_here(h, n):
        a, b = x_target(h, n)
        return jnp.logical_and(a == s, b == q)

    def x_local(h, n):
        return pltpu.make_async_copy(ns.at[h, n // 2], x_rows(h, s), x_recv.at[h, s // 2])

    def direct(h, m):
        return 2 * m + lax.rem(c + h, 2)

    def x_arrival(h, m):
        rows = x_rows(h, direct(h, m))
        return pltpu.make_async_copy(rows, rows, x_recv.at[h, m])

    def x_forward(h, m):
        rows = x_rows(h, direct(h, m))
        return remote(rows, rows, xf_send.at[h, m], xf_recv.at[h, m], mate)

    def x_forwarded(h, m):
        rows = x_rows(h, 2 * m + lax.rem(c + h + 1, 2))
        return remote(rows, rows, xf_send.at[h, m], xf_recv.at[h, m], mate)

    def states(h):
        each(1, SEQ_DEVS, lambda k: e1_arrival(h, k).wait_recv())
        for i in range(4):
            shifted = e1[h] + tes[pl.ds(4 * q + i, 1), :]
            if i:
                shifted = shifted + scale * dr1[h, i - 1]
            mean = jnp.mean(shifted * shifted, axis=1, keepdims=True)
            ns[h, i] = (shifted * lax.rsqrt(mean + NORM_EPS)).astype(BF16)
            for n in (2 * i, 2 * i + 1):
                @pl.when(is_here(h, n))
                def _():
                    x_local(h, n).start()

                @pl.when(jnp.logical_not(is_here(h, n)))
                def _():
                    x_copy(h, n).start()

    @pl.when(q != owner_q)
    def _():
        for h in range(2):
            sb_copy_in = remote(stb.at[h], stb.at[h], sb_send.at[h, 0], sb_recv.at[h], here)
            sb_copy_in.wait_recv()

    wo_third()
    drift1(0)
    drift1(1)
    scan1(0)
    scan1(1)
    states(0)
    states(1)

    for n in range(3):
        w2_copy(n).wait()

    def project(h, sub):
        rows = pl.ds(h * 8 * half + sub * 4 * half, 4 * half)

        def columns(n):
            cols = pl.ds(aligned(n * gw, gw), gw)
            f = jnp.where(n == 0, QUERY_SCALE, 1.0)
            qkv2[rows, cols] = (jnp.dot(xs[rows, :], w2[:, cols], preferred_element_type=F32) * f).astype(BF16)

        each(0, 3, columns)

    for h in range(2):
        for sub in range(2):
            for m in range(4 * sub, 4 * sub + 4):
                x_arrival(h, m).wait()
                x_forward(h, m).start()
        for sub in range(2):
            for m in range(4 * sub, 4 * sub + 4):
                x_forwarded(h, m).wait_recv()
            project(h, sub)

    def a2_block(h, who):
        yy, cc = who // 2, who % 2
        return recv2.at[h, pl.ds(aligned((yy // 2) * half, half), half),
                        pl.ds(aligned(((yy % 2) * 2 + cc) * gw, gw), gw)]

    def att2_rows(h, who):
        return att2.at[pl.ds(aligned(h * 8 * half + who * half, half), half)]

    def a2_copy(h, k):
        dest = seq_peer(k)
        return remote(att2_rows(h, dest), a2_block(h, q), a2_send.at[h, k - 1], a2_recv.at[h, k - 1], (s, dest))

    def a2_arrival(h, k):
        return remote(att2_rows(h, q), a2_block(h, seq_peer(SEQ_DEVS - k)),
                      a2_send.at[h, k - 1], a2_recv.at[h, k - 1], here)

    def a2_own(h):
        return pltpu.make_async_copy(att2_rows(h, q), a2_block(h, q), a2_sem.at[h])

    for h in range(2):
        rows = pl.ds(h * 8 * half, 8 * half)

        def cols(p, head):
            return pl.ds(aligned(p * gw + head * HEAD_SIZE, HEAD_SIZE), HEAD_SIZE)

        def scores2(head):
            return score(qkv2[rows, cols(0, head)], qkv2[:, cols(1, head)])

        def mix2(head, scores):
            att2[rows, cols(0, head)] = mix(scores, qkv2[:, cols(2, head)])

        score_a[...] = scores2(0)
        each(0, 2, two_by_two(scores2, mix2))
        each(1, SEQ_DEVS, lambda k: a2_copy(h, k).start())
        a2_own(h).start()

    def p2_copy(h, k):
        dest = step_peer(k)
        return remote(piece(bs2.at[h], dest), pr2.at[h, s], p2_send.at[h, k - 1], p2_recv.at[h, k - 1], (dest, q))

    def p2_arrival(h, k):
        return remote(piece(bs2.at[h], s), pr2.at[h, step_peer(STEP_DEVS - k)],
                      p2_send.at[h, k - 1], p2_recv.at[h, k - 1], here)

    def e2_copy(h, k):
        dest = step_peer(k)
        return remote(pe2.at[h, dest], piece(e2.at[h], s), e2_send.at[h, k - 1], e2_recv.at[h, k - 1], (dest, q))

    def e2_arrival(h, k):
        return remote(pe2.at[h, s], piece(e2.at[h], step_peer(STEP_DEVS - k)),
                      e2_send.at[h, k - 1], e2_recv.at[h, k - 1], here)

    def drift2(h):
        a2_own(h).wait()
        each(1, SEQ_DEVS, lambda k: a2_arrival(h, k).wait_recv())

        def tile(n):
            cols = pl.ds(aligned(n * 256, 256), 256)
            rows = jnp.dot(recv2[h], wo[:, cols], preferred_element_type=F32)
            first = rows[0:half]
            total = first + rows[half:]
            dr2[h, 0, :, cols] = first
            dr2[h, 1, :, cols] = total
            bs2[h, :, cols] = total.astype(BF16)

        each(0, width // 256, tile)
        each(1, STEP_DEVS, lambda k: p2_copy(h, k).start())
        pr2[h, s] = piece(bs2.at[h], s)[...]

    def scan2(h):
        each(1, STEP_DEVS, lambda k: p2_arrival(h, k).wait_recv())
        total = jnp.zeros((16, lane4), F32)
        for k in range(STEP_DEVS):
            pe2[h, k] = total
            total = total + pr2[h, k].astype(F32)
        each(1, STEP_DEVS, lambda k: e2_copy(h, k).start())
        piece(e2.at[h], s)[...] = pe2[h, s]

    def finish(h):
        each(1, STEP_DEVS, lambda k: e2_arrival(h, k).wait_recv())
        for i in range(2):
            for b in range(2):
                rows = slice(part * b, part * (b + 1))
                out_ref[i, half * b + part * h:half * b + part * (h + 1), :] = e2[h, rows, :] + dr2[h, i, rows, :]

    drift2(0)
    drift2(1)
    scan2(0)
    scan2(1)
    finish(0)
    finish(1)

    each(1, STEP_DEVS, lambda k: te_copy(k).wait_send())
    for dy in range(1, 4):
        sw_copy(dy).wait_send()
        for n in range(4):
            wn_copy(dy, n).wait_send()
    for dy in range(4):
        sw_forward(dy).wait_send()
    for n in range(8):
        wf_copy(n).wait_send()
    for r in range(2):
        wy_copy(1 + 2 * r).wait_send()
        wr_copy(r).wait_send()
    each(1, SEQ_DEVS, lambda k: rt_copy(k).wait_send())

    @pl.when(q == owner_q)
    def _():
        for h in range(2):
            each(1, SEQ_DEVS, lambda k: sb_copy(k, h).wait_send())

    for h in range(2):
        for k in range(1, SEQ_DEVS):
            p1_copy(h, k).wait_send()
            e1_copy(h, k).wait_send()
            a2_copy(h, k).wait_send()
        for k in range(1, STEP_DEVS):
            a1_copy(h, k).wait_send()
            p2_copy(h, k).wait_send()
            e2_copy(h, k).wait_send()
        for n in range(8):
            @pl.when(jnp.logical_not(is_here(h, n)))
            def _():
                x_copy(h, n).wait_send()
        for m in range(8):
            x_forward(h, m).wait_send()


def on_device(start_state, timesteps, qkv_weight, out_weight):
    tok, width = start_state.shape
    half, part, lane4 = tok // 2, tok // 4, width // 4
    te = embed(timesteps, width)
    dma = pltpu.SemaphoreType.DMA
    vmem = pl.BlockSpec(memory_space=pltpu.VMEM)
    hbm = pl.BlockSpec(memory_space=pl.ANY)
    sums = pl.pallas_call(
        kernel,
        out_shape=jax.ShapeDtypeStruct((2, tok, width), F32),
        in_specs=[vmem, hbm, hbm, hbm],
        out_specs=vmem,
        scratch_shapes=[
            pltpu.VMEM((width, 3 * HEAD_SIZE), BF16),
            pltpu.VMEM((width, 3 * INNER // 4), BF16),
            pltpu.VMEM((INNER, width), BF16),
            pltpu.VMEM((tok, width), F32),
            pltpu.VMEM((STEP_DEVS, 2, width), F32),
            pltpu.VMEM((STEPS, width), F32),
            pltpu.VMEM((SEQ_DEVS, tok, 3 * HEAD_SIZE), BF16),
            pltpu.VMEM((SEQ_DEVS, STEPS, tok), F32),
            pltpu.VMEM((STEPS, 3 * HEAD_SIZE), F32),
            pltpu.VMEM((4, SEQ_DEVS, tok, 3 * HEAD_SIZE), BF16),
            pltpu.VMEM((2, STEP_DEVS, 4 * part, HEAD_SIZE), BF16),
            pltpu.VMEM((2, 4 * part, INNER), BF16),
            pltpu.VMEM((2, 4, part, width), F32),
            pltpu.VMEM((2, part, width), BF16),
            pltpu.VMEM((2, SEQ_DEVS, 16, lane4), BF16),
            pltpu.VMEM((2, SEQ_DEVS, 16, lane4), F32),
            pltpu.VMEM((2, part, width), F32),
            pltpu.VMEM((2, 16, lane4), F32),
            pltpu.VMEM((2, 4, part, width), BF16),
            pltpu.VMEM((8 * tok, width), BF16),
            pltpu.VMEM((8 * tok, 3 * INNER // 4), BF16),
            pltpu.VMEM((8 * tok, INNER // 4), BF16),
            pltpu.VMEM((2, tok, INNER), BF16),
            pltpu.VMEM((2, 2, half, width), F32),
            pltpu.VMEM((2, half, width), BF16),
            pltpu.VMEM((2, STEP_DEVS, 16, lane4), BF16),
            pltpu.VMEM((2, STEP_DEVS, 16, lane4), F32),
            pltpu.VMEM((2, half, width), F32),
            pltpu.VMEM((8 * half, 8 * tok), F32),
            pltpu.VMEM((8 * half, 8 * tok), F32),
            dma((3,)), dma((3,)), dma, dma((4,)),
            dma((15,)), dma((15,)), dma((3,)), dma((3,)), dma((4,)), dma((4,)), dma((7,)), dma((7,)),
            dma((2, 7)), dma((2,)),
            dma((3,)), dma((3,)), dma((2,)), dma((2,)), dma((3, 4)), dma((3, 4)), dma((8,)), dma((8,)),
            dma((2, 15)), dma((2, 15)), dma((2, 7)), dma((2, 7)), dma((2, 7)), dma((2, 7)),
            dma((2, 8)), dma((2, 8)), dma((2, 8)), dma((2, 8)),
            dma((2, 7)), dma((2, 7)), dma((2,)), dma((2, 15)), dma((2, 15)), dma((2, 15)), dma((2, 15)),
        ],
        compiler_params=pltpu.CompilerParams(
            collective_id=0, has_side_effects=True, vmem_limit_bytes=58 * 1024 * 1024),
        name="picard",
    )(te, start_state, qkv_weight, out_weight)
    return start_state[None] + (1.0 / STEPS) * sums


def solution(mesh):
    return jax.shard_map(
        on_device,
        mesh=mesh,
        in_specs=(P("seq", None), P("step"), P(), P("seq", None)),
        out_specs=P("step", "seq", None),
        check_vma=False,
    )
```

```python
import functools
import math

import jax
import jax.numpy as jnp
from jax import lax
from jax.experimental import pallas as pl
from jax.experimental.pallas import tpu as pltpu
from jax.sharding import PartitionSpec as P

HEAD_SIZE = 128
HEADS = 16
INNER = HEADS * HEAD_SIZE
STEP_DEVS = 16
SEQ_DEVS = 8
STEPS = 32
NORM_EPS = 1e-06
MESH = pl.DeviceIdType.MESH
F32 = jnp.float32
BF16 = jnp.bfloat16
QUERY_SCALE = math.log2(math.e) / math.sqrt(HEAD_SIZE)


def embed(step_index, model_width):
    half_width = model_width // 2
    frequency = jnp.exp(-math.log(10000.0) * jnp.arange(half_width, dtype=F32) / half_width)
    angles = step_index.astype(F32)[:, None] * frequency[None, :]
    return jnp.concatenate([jnp.sin(angles), jnp.cos(angles)], axis=1)


def remote(src, dst, send_sem, recv_sem, device):
    return pltpu.make_async_remote_copy(
        src_ref=src, dst_ref=dst, send_sem=send_sem, recv_sem=recv_sem,
        device_id=device, device_id_type=MESH)


def aligned(value, by):
    return pl.multiple_of(value, by)


def each(first, last, body):
    def step(k, carry):
        body(k)
        return carry

    lax.fori_loop(first, last, step, 0)


def split_dot(values, weights):
    high = values.astype(BF16)
    low = (values - high.astype(F32)).astype(BF16)
    return (jnp.dot(high, weights, preferred_element_type=F32)
            + jnp.dot(low, weights, preferred_element_type=F32))


def score(queries, keys):
    return lax.dot_general(queries, keys, (((1,), (1,)), ((), ())), preferred_element_type=F32)


def mix(scores, values):
    expo = jnp.exp2(scores - jnp.max(scores, axis=1, keepdims=True))
    total = jnp.sum(expo, axis=1, keepdims=True)
    mixed = jnp.dot(expo.astype(BF16), values, preferred_element_type=F32)
    return (mixed / total).astype(BF16)


def kernel(
    te_ref, start_ref, wqkv_ref, wout_ref,
    out_ref,
    w1, w2, wo, st, tea, tes, swb, rtb, tew, qkv1, att1, recv1, dr1, bs1, pr1, pe1, e1, stb, ns,
    xs, qkv2, att2, recv2, dr2, bs2, pr2, pe2, e2, score_a, score_b,
    w1_sem, w2_sem, wo_sem, st_sem,
    te_send, te_recv, sw_send, sw_recv, swf_send, swf_recv, rt_send, rt_recv, sb_send, sb_recv,
    wy_send, wy_recv, wr_send, wr_recv, wn_send, wn_recv, wf_send, wf_recv,
    a1_send, a1_recv, p1_send, p1_recv, e1_send, e1_recv,
    x_send, x_recv, xf_send, xf_recv,
    a2_send, a2_recv, a2_sem, p2_send, p2_recv, e2_send, e2_recv,
):
    tok, width = start_ref.shape
    half, part = tok // 2, tok // 4
    lane4 = width // 4
    orow = wout_ref.shape[0]
    s = lax.axis_index("step")
    q = lax.axis_index("seq")
    y, c = q // 2, q % 2
    parity = y // 2
    group = (y % 2) * 2 + c
    gw = INNER // 4
    scale = 1.0 / STEPS
    here = (s, q)
    mate = (s, 2 * y + 1 - c)

    def chip(dy):
        return lax.rem(y + dy, 4)

    def step_peer(k):
        return lax.rem(s + k, STEP_DEVS)

    def seq_peer(k):
        return lax.rem(q + k, SEQ_DEVS)

    def w1_copy(n):
        return pltpu.make_async_copy(
            wqkv_ref.at[:, pl.ds(aligned(n * INNER + s * HEAD_SIZE, 128), HEAD_SIZE)],
            w1.at[:, pl.ds(n * HEAD_SIZE, HEAD_SIZE)], w1_sem.at[n])

    def w2_copy(n):
        return pltpu.make_async_copy(
            wqkv_ref.at[:, pl.ds(aligned(n * INNER + group * gw, 128), gw)],
            w2.at[:, pl.ds(n * gw, gw)], w2_sem.at[n])

    def st_copy(n):
        h, b = n // 2, n % 2
        return pltpu.make_async_copy(
            start_ref.at[pl.ds(half * b + part * h, part)],
            st.at[pl.ds(half * h + part * b, part)], st_sem.at[n])

    def wo_rows(owner, first, count):
        return wo.at[pl.ds(aligned(owner * orow + first, 16), count)]

    wo_own = pltpu.make_async_copy(wout_ref, wo_rows(q, 0, orow), wo_sem)
    for n in range(4):
        st_copy(n).start()
    for n in range(3):
        w1_copy(n).start()
    wo_own.start()

    barrier = pltpu.get_barrier_semaphore()
    each(1, STEP_DEVS, lambda k: pl.semaphore_signal(
        barrier, inc=1, device_id=(step_peer(k), q), device_id_type=MESH))
    each(1, SEQ_DEVS, lambda k: pl.semaphore_signal(
        barrier, inc=1, device_id=(s, seq_peer(k)), device_id_type=MESH))

    for n in range(4):
        st_copy(n).wait()
    for n in range(3):
        w1_copy(n).wait()
    lane = lax.broadcasted_iota(jnp.int32, (1, 3 * HEAD_SIZE), 1)
    factor = jnp.where(lane < HEAD_SIZE, QUERY_SCALE, 1.0)
    swb[q] = (split_dot(st[...], w1[...]) * factor).astype(BF16)
    pl.semaphore_wait(barrier, STEP_DEVS - 1 + SEQ_DEVS - 1)

    def te_copy(k):
        return remote(te_ref, tea.at[s], te_send.at[k - 1], te_recv.at[k - 1], (step_peer(k), q))

    def te_arrival(k):
        return remote(te_ref, tea.at[step_peer(STEP_DEVS - k)], te_send.at[k - 1], te_recv.at[k - 1], here)

    each(1, STEP_DEVS, lambda k: te_copy(k).start())
    tea[s] = te_ref[...]

    def sw_copy(dy):
        return remote(swb.at[q], swb.at[q], sw_send.at[dy - 1], sw_recv.at[dy - 1], (s, 2 * chip(dy) + c))

    def sw_arrival(dy):
        return remote(swb.at[q], swb.at[2 * chip(4 - dy) + c], sw_send.at[dy - 1], sw_recv.at[dy - 1], here)

    def sw_forward(dy):
        owner = 2 * chip(4 - dy) + c
        return remote(swb.at[owner], swb.at[owner], swf_send.at[dy % 4], swf_recv.at[dy % 4], mate)

    def sw_forwarded(dy):
        owner = 2 * chip(4 - dy) + 1 - c
        return remote(swb.at[owner], swb.at[owner], swf_send.at[dy % 4], swf_recv.at[dy % 4], mate)

    for dy in (2, 1, 3):
        sw_copy(dy).start()
    sw_forward(0).start()

    zx = (s // 4 + s) % 2
    hrow, qrow, erow = orow // 2, orow // 4, orow // 8

    def wo_of(n, core, first, count):
        return wo_rows(2 * chip(n) + core, first, count)

    def wy_copy(dy):
        return remote(wout_ref.at[pl.ds(aligned(zx * hrow, 16), hrow)], wo_rows(q, zx * hrow, hrow),
                      wy_send.at[dy - 1], wy_recv.at[dy - 1], (s, 2 * chip(dy) + c))

    def wy_arrival(dy):
        rows = wo_of(4 - dy, c, zx * hrow, hrow)
        return remote(rows, rows, wy_send.at[dy - 1], wy_recv.at[dy - 1], here)

    def wr_copy(r):
        rows = wo_of(1 if r else 3, c, zx * hrow + r * qrow, qrow)
        return remote(rows, rows, wr_send.at[r], wr_recv.at[r], (s, 2 * chip(3 if r else 1) + c))

    def wr_arrival(r):
        rows = wo_of(2, c, zx * hrow + r * qrow, qrow)
        return remote(rows, rows, wr_send.at[r], wr_recv.at[r], here)

    def neighbour(n):
        if n < 2:
            return step_peer(4 if n == 0 else STEP_DEVS - 4)
        return (s // 4) * 4 + lax.rem(s + (1 if n == 2 else 3), 4)

    def wn_copy(b, n):
        rows = wo_of(b, c, zx * hrow + n * erow, erow)
        return remote(rows, rows, wn_send.at[b - 1, n], wn_recv.at[b - 1, n], (neighbour(n), q))

    def wn_arrival(b, n):
        rows = wo_of(b, c, (1 - zx) * hrow + n * erow, erow)
        return remote(rows, rows, wn_send.at[b - 1, n], wn_recv.at[b - 1, n], here)

    def wf_rows(n, core):
        if n == 0:
            return wo_rows(2 * y + core, 0, orow)
        if n < 3:
            return wo_of(1 if n == 1 else 3, core, zx * hrow, hrow)
        if n < 5:
            return wo_of(2, core, zx * hrow + (n - 3) * qrow, qrow)
        return wo_of(n - 4, core, (1 - zx) * hrow, hrow)

    def wf_copy(n):
        return remote(wf_rows(n, c), wf_rows(n, c), wf_send.at[n], wf_recv.at[n], mate)

    def wf_arrival(n):
        return remote(wf_rows(n, 1 - c), wf_rows(n, 1 - c), wf_send.at[n], wf_recv.at[n], mate)

    def wo_first():
        for dy in (1, 3):
            wy_arrival(dy).wait_recv()
            wr_copy(0 if dy == 1 else 1).start()
            for n in range(4):
                wn_copy(4 - dy, n).start()
            wf_copy(2 if dy == 1 else 1).start()

    def wo_second():
        for r in range(2):
            wr_arrival(r).wait_recv()
            wn_copy(2, 2 * r).start()
            wn_copy(2, 2 * r + 1).start()
            wf_copy(3 + r).start()

    def wo_middle():
        for b in (3, 1):
            for n in range(4):
                wn_arrival(b, n).wait_recv()
            wf_copy(4 + b).start()

    def wo_third():
        for n in range(4):
            wn_arrival(2, n).wait_recv()
        wf_copy(6).start()
        for n in range(8):
            wf_arrival(n).wait_recv()


    owner_q = s // 2
    block = s % 2

    def sb_src(h, who):
        return st.at[pl.ds(aligned(half * h + part * block + (who // 4) * 16, 8), 16),
                     pl.ds(aligned((who % 4) * lane4, 128), lane4)]

    def sb_copy(k, h):
        return remote(sb_src(h, seq_peer(k)), stb.at[h], sb_send.at[h, k - 1], sb_recv.at[h], (s, seq_peer(k)))

    @pl.when(q == owner_q)
    def _():
        for h in range(2):
            each(1, SEQ_DEVS, lambda k: sb_copy(k, h).start())
            stb[h] = sb_src(h, q)[...]

    for n in range(3):
        w2_copy(n).start()

    each(1, STEP_DEVS, lambda k: te_arrival(k).wait_recv())
    for n in range(STEP_DEVS):
        tes[2 * n:2 * n + 2, :] = tea[n]
    own = st[...]
    transposed = (((1,), (1,)), ((), ()))

    def parts(values):
        high = values.astype(BF16)
        return high, (values - high.astype(F32)).astype(BF16)

    def dot_t(a, b):
        return lax.dot_general(a, b, transposed, preferred_element_type=F32)

    own_parts, te_parts, square_parts = parts(own), parts(tes[...]), parts(own * own)
    cross = dot_t(te_parts[0], own_parts[0]) + dot_t(te_parts[1], own_parts[0]) + dot_t(te_parts[0], own_parts[1])
    one_row = jnp.ones((16, width), BF16)
    squares = (dot_t(one_row, square_parts[0]) + dot_t(one_row, square_parts[1]))[0:1]
    step_squares = jnp.sum(tes[...] * tes[...], axis=1, keepdims=True)
    mean_square = jnp.maximum((squares + 2.0 * cross + step_squares) * (1.0 / width), 0.0)
    rtb[q] = lax.rsqrt(mean_square + NORM_EPS)

    def rt_copy(k):
        return remote(rtb.at[q], rtb.at[q], rt_send.at[k - 1], rt_recv.at[k - 1], (s, seq_peer(k)))

    def rt_arrival(k):
        return remote(rtb.at[q], rtb.at[seq_peer(SEQ_DEVS - k)], rt_send.at[k - 1], rt_recv.at[k - 1], here)

    each(1, SEQ_DEVS, lambda k: rt_copy(k).start())
    tew[...] = split_dot(tes[...], w1[...]) * factor

    for dy in (1, 3, 2):
        sw_arrival(dy).wait_recv()
        sw_forward(dy).start()
    each(1, SEQ_DEVS, lambda k: rt_arrival(k).wait_recv())
    for dy in range(4):
        sw_forwarded(dy).wait_recv()

    for dy in (1, 3):
        wy_copy(dy).start()

    pick_row = lax.broadcasted_iota(jnp.int32, (STEPS, 4 * HEAD_SIZE), 0)
    pick_lane = lax.broadcasted_iota(jnp.int32, (STEPS, 4 * HEAD_SIZE), 1)
    pick = (pick_row == 4 * q + pick_lane // HEAD_SIZE).astype(BF16)

    def build(b):
        scales = sum(lax.dot_general(rows, pick, (((0,), (0,)), ((), ())), preferred_element_type=F32)
                     for rows in parts(rtb[b]))
        base = swb[b].astype(F32)
        for i in range(4):
            rows = scales[:, i * HEAD_SIZE:(i + 1) * HEAD_SIZE]
            step_row = tew[pl.ds(4 * q + i, 1), :]
            for n3 in range(3):
                cols = slice(n3 * HEAD_SIZE, (n3 + 1) * HEAD_SIZE)
                qkv1[i, b, :, cols] = ((base[:, cols] + step_row[:, cols]) * rows).astype(BF16)

    each(0, SEQ_DEVS, build)

    def two_by_two(scores_of, mix_of):
        def pair(n):
            score_b[...] = scores_of(2 * n + 1)
            mix_of(2 * n, score_a[...])
            score_a[...] = scores_of(jnp.minimum(2 * n + 2, 3))
            mix_of(2 * n + 1, score_b[...])

        return pair

    def a1_copy(h, k):
        return remote(att1.at[h, step_peer(k)], recv1.at[h, :, pl.ds(aligned(s * HEAD_SIZE, 128), HEAD_SIZE)],
                      a1_send.at[h, k - 1], a1_recv.at[h, k - 1], (step_peer(k), q))

    def a1_arrival(h, k):
        src = step_peer(STEP_DEVS - k)
        return remote(att1.at[h, s], recv1.at[h, :, pl.ds(aligned(src * HEAD_SIZE, 128), HEAD_SIZE)],
                      a1_send.at[h, k - 1], a1_recv.at[h, k - 1], here)

    for h in range(2):
        def scores1(i):
            queries = qkv1[i, :, half * h:half * (h + 1), 0:HEAD_SIZE].reshape(8 * half, HEAD_SIZE)
            return score(queries, qkv1[i, :, :, HEAD_SIZE:2 * HEAD_SIZE].reshape(8 * tok, HEAD_SIZE))

        def mix1(i, scores):
            values = qkv1[i, :, :, 2 * HEAD_SIZE:3 * HEAD_SIZE].reshape(8 * tok, HEAD_SIZE)
            att1[h, :, pl.ds(aligned(i * part, part), part), :] = mix(scores, values).reshape(
                STEP_DEVS, part, HEAD_SIZE)

        attend1 = two_by_two(scores1, mix1)
        score_a[...] = scores1(0)
        if h == 0:
            wo_own.wait()
            wf_copy(0).start()
            each(0, 1, attend1)
            wo_first()
            each(1, 2, attend1)
        else:
            each(0, 1, attend1)
            wo_second()
            each(1, 2, attend1)
        each(1, STEP_DEVS, lambda k: a1_copy(h, k).start())
        recv1[h, :, pl.ds(aligned(s * HEAD_SIZE, 128), HEAD_SIZE)] = att1[h, s]

    wo_middle()

    def piece(ref, who):
        return ref.at[pl.ds(aligned((who // 4) * 16, 16), 16), pl.ds(aligned((who % 4) * lane4, 128), lane4)]

    def p1_copy(h, k):
        dest = seq_peer(k)
        return remote(piece(bs1.at[h], dest), pr1.at[h, q], p1_send.at[h, k - 1], p1_recv.at[h, k - 1], (s, dest))

    def p1_arrival(h, k):
        return remote(piece(bs1.at[h], q), pr1.at[h, seq_peer(SEQ_DEVS - k)],
                      p1_send.at[h, k - 1], p1_recv.at[h, k - 1], here)

    def e1_copy(h, k):
        dest = seq_peer(k)
        return remote(pe1.at[h, dest], piece(e1.at[h], q), e1_send.at[h, k - 1], e1_recv.at[h, k - 1], (s, dest))

    def e1_arrival(h, k):
        return remote(pe1.at[h, q], piece(e1.at[h], seq_peer(SEQ_DEVS - k)),
                      e1_send.at[h, k - 1], e1_recv.at[h, k - 1], here)

    def drift1(h):
        each(1, STEP_DEVS, lambda k: a1_arrival(h, k).wait_recv())

        def tile(n):
            cols = pl.ds(aligned(n * 256, 256), 256)
            rows = jnp.dot(recv1[h], wo[:, cols], preferred_element_type=F32)
            total = rows[0:part]
            dr1[h, 0, :, cols] = total
            for i in range(1, 4):
                total = total + rows[i * part:(i + 1) * part]
                dr1[h, i, :, cols] = total
            bs1[h, :, cols] = total.astype(BF16)

        each(0, width // 256, tile)
        each(1, SEQ_DEVS, lambda k: p1_copy(h, k).start())
        pr1[h, q] = piece(bs1.at[h], q)[...]

    def scan1(h):
        each(1, SEQ_DEVS, lambda k: p1_arrival(h, k).wait_recv())
        total = jnp.zeros((16, lane4), F32)
        for k in range(SEQ_DEVS):
            pe1[h, k] = stb[h] + scale * total
            total = total + pr1[h, k].astype(F32)
        each(1, SEQ_DEVS, lambda k: e1_copy(h, k).start())
        piece(e1.at[h], q)[...] = pe1[h, q]

    def x_rows(h, who):
        return xs.at[pl.ds(aligned(h * 8 * half + who * part, part), part)]

    def x_target(h, n):
        i, e = n // 2, n % 2
        return 2 * q + i // 2, 2 * (2 * (i % 2) + e) + lax.rem(s + h, 2)

    def x_copy(h, n):
        return remote(ns.at[h, n // 2], x_rows(h, s), x_send.at[h, n], x_recv.at[h, s // 2], x_target(h, n))

    def is_here(h, n):
        a, b = x_target(h, n)
        return jnp.logical_and(a == s, b == q)

    def x_local(h, n):
        return pltpu.make_async_copy(ns.at[h, n // 2], x_rows(h, s), x_recv.at[h, s // 2])

    def direct(h, m):
        return 2 * m + lax.rem(c + h, 2)

    def x_arrival(h, m):
        rows = x_rows(h, direct(h, m))
        return pltpu.make_async_copy(rows, rows, x_recv.at[h, m])

    def x_forward(h, m):
        rows = x_rows(h, direct(h, m))
        return remote(rows, rows, xf_send.at[h, m], xf_recv.at[h, m], mate)

    def x_forwarded(h, m):
        rows = x_rows(h, 2 * m + lax.rem(c + h + 1, 2))
        return remote(rows, rows, xf_send.at[h, m], xf_recv.at[h, m], mate)

    def states(h):
        each(1, SEQ_DEVS, lambda k: e1_arrival(h, k).wait_recv())
        for i in range(4):
            shifted = e1[h] + tes[pl.ds(4 * q + i, 1), :]
            if i:
                shifted = shifted + scale * dr1[h, i - 1]
            mean = jnp.mean(shifted * shifted, axis=1, keepdims=True)
            ns[h, i] = (shifted * lax.rsqrt(mean + NORM_EPS)).astype(BF16)
            for n in (2 * i, 2 * i + 1):
                @pl.when(is_here(h, n))
                def _():
                    x_local(h, n).start()

                @pl.when(jnp.logical_not(is_here(h, n)))
                def _():
                    x_copy(h, n).start()

    @pl.when(q != owner_q)
    def _():
        for h in range(2):
            sb_copy_in = remote(stb.at[h], stb.at[h], sb_send.at[h, 0], sb_recv.at[h], here)
            sb_copy_in.wait_recv()

    wo_third()
    drift1(0)
    drift1(1)
    scan1(0)
    scan1(1)
    states(0)
    states(1)

    for n in range(3):
        w2_copy(n).wait()

    def project(h):
        rows = pl.ds(h * 8 * half, 8 * half)

        def columns(n):
            cols = pl.ds(aligned(n * gw, gw), gw)
            f = jnp.where(n == 0, QUERY_SCALE, 1.0)
            qkv2[rows, cols] = (jnp.dot(xs[rows, :], w2[:, cols], preferred_element_type=F32) * f).astype(BF16)

        each(0, 3, columns)

    for h in range(2):
        for m in range(8):
            x_arrival(h, m).wait()
            x_forward(h, m).start()
        for m in range(8):
            x_forwarded(h, m).wait_recv()
        project(h)

    def a2_block(h, p, who):
        yy, cc = who // 2, who % 2
        return recv2.at[h, pl.ds(aligned((yy // 2) * half, half), half),
                        pl.ds(aligned(((yy % 2) * 2 + cc) * gw + p * (gw // 2), gw // 2), gw // 2)]

    def att2_rows(h, p, who):
        return att2.at[pl.ds(aligned(h * 8 * half + who * half, half), half), pl.ds(p * (gw // 2), gw // 2)]

    def a2_copy(h, p, k):
        dest = seq_peer(k)
        return remote(att2_rows(h, p, dest), a2_block(h, p, q), a2_send.at[h, p, k - 1], a2_recv.at[h, p, k - 1],
                      (s, dest))

    def a2_arrival(h, p, k):
        return remote(att2_rows(h, p, q), a2_block(h, p, seq_peer(SEQ_DEVS - k)),
                      a2_send.at[h, p, k - 1], a2_recv.at[h, p, k - 1], here)

    def a2_own(h, p):
        return pltpu.make_async_copy(att2_rows(h, p, q), a2_block(h, p, q), a2_sem.at[h, p])

    for h in range(2):
        rows = pl.ds(h * 8 * half, 8 * half)

        def cols(p, head):
            return pl.ds(aligned(p * gw + head * HEAD_SIZE, HEAD_SIZE), HEAD_SIZE)

        def scores2(head):
            return score(qkv2[rows, cols(0, head)], qkv2[:, cols(1, head)])

        def mix2(head, scores):
            att2[rows, cols(0, head)] = mix(scores, qkv2[:, cols(2, head)])

        score_a[...] = scores2(0)
        for p in range(2):
            each(p, p + 1, two_by_two(scores2, mix2))
            each(1, SEQ_DEVS, lambda k: a2_copy(h, p, k).start())
            a2_own(h, p).start()

    def p2_copy(h, k):
        dest = step_peer(k)
        return remote(piece(bs2.at[h], dest), pr2.at[h, s], p2_send.at[h, k - 1], p2_recv.at[h, k - 1], (dest, q))

    def p2_arrival(h, k):
        return remote(piece(bs2.at[h], s), pr2.at[h, step_peer(STEP_DEVS - k)],
                      p2_send.at[h, k - 1], p2_recv.at[h, k - 1], here)

    def e2_copy(h, k):
        dest = step_peer(k)
        return remote(pe2.at[h, dest], piece(e2.at[h], s), e2_send.at[h, k - 1], e2_recv.at[h, k - 1], (dest, q))

    def e2_arrival(h, k):
        return remote(pe2.at[h, s], piece(e2.at[h], step_peer(STEP_DEVS - k)),
                      e2_send.at[h, k - 1], e2_recv.at[h, k - 1], here)

    def drift2(h):
        for p in range(2):
            a2_own(h, p).wait()
            each(1, SEQ_DEVS, lambda k: a2_arrival(h, p, k).wait_recv())

        def tile(n):
            cols = pl.ds(aligned(n * 256, 256), 256)
            rows = jnp.dot(recv2[h], wo[:, cols], preferred_element_type=F32)
            first = rows[0:half]
            total = first + rows[half:]
            dr2[h, 0, :, cols] = first
            dr2[h, 1, :, cols] = total
            bs2[h, :, cols] = total.astype(BF16)

        each(0, width // 256, tile)
        each(1, STEP_DEVS, lambda k: p2_copy(h, k).start())
        pr2[h, s] = piece(bs2.at[h], s)[...]

    def scan2(h):
        each(1, STEP_DEVS, lambda k: p2_arrival(h, k).wait_recv())
        total = jnp.zeros((16, lane4), F32)
        for k in range(STEP_DEVS):
            pe2[h, k] = total
            total = total + pr2[h, k].astype(F32)
        each(1, STEP_DEVS, lambda k: e2_copy(h, k).start())
        piece(e2.at[h], s)[...] = pe2[h, s]

    def finish(h):
        each(1, STEP_DEVS, lambda k: e2_arrival(h, k).wait_recv())
        for i in range(2):
            for b in range(2):
                rows = slice(part * b, part * (b + 1))
                out_ref[i, half * b + part * h:half * b + part * (h + 1), :] = e2[h, rows, :] + dr2[h, i, rows, :]

    drift2(0)
    drift2(1)
    scan2(0)
    scan2(1)
    finish(0)
    finish(1)

    each(1, STEP_DEVS, lambda k: te_copy(k).wait_send())
    for dy in range(1, 4):
        sw_copy(dy).wait_send()
        for n in range(4):
            wn_copy(dy, n).wait_send()
    for dy in range(4):
        sw_forward(dy).wait_send()
    for n in range(8):
        wf_copy(n).wait_send()
    for r in range(2):
        wy_copy(1 + 2 * r).wait_send()
        wr_copy(r).wait_send()
    each(1, SEQ_DEVS, lambda k: rt_copy(k).wait_send())

    @pl.when(q == owner_q)
    def _():
        for h in range(2):
            each(1, SEQ_DEVS, lambda k: sb_copy(k, h).wait_send())

    for h in range(2):
        for k in range(1, SEQ_DEVS):
            p1_copy(h, k).wait_send()
            e1_copy(h, k).wait_send()
            for p in range(2):
                a2_copy(h, p, k).wait_send()
        for k in range(1, STEP_DEVS):
            a1_copy(h, k).wait_send()
            p2_copy(h, k).wait_send()
            e2_copy(h, k).wait_send()
        for n in range(8):
            @pl.when(jnp.logical_not(is_here(h, n)))
            def _():
                x_copy(h, n).wait_send()
        for m in range(8):
            x_forward(h, m).wait_send()


def on_device(start_state, timesteps, qkv_weight, out_weight):
    tok, width = start_state.shape
    half, part, lane4 = tok // 2, tok // 4, width // 4
    te = embed(timesteps, width)
    dma = pltpu.SemaphoreType.DMA
    vmem = pl.BlockSpec(memory_space=pltpu.VMEM)
    hbm = pl.BlockSpec(memory_space=pl.ANY)
    sums = pl.pallas_call(
        kernel,
        out_shape=jax.ShapeDtypeStruct((2, tok, width), F32),
        in_specs=[vmem, hbm, hbm, hbm],
        out_specs=vmem,
        scratch_shapes=[
            pltpu.VMEM((width, 3 * HEAD_SIZE), BF16),
            pltpu.VMEM((width, 3 * INNER // 4), BF16),
            pltpu.VMEM((INNER, width), BF16),
            pltpu.VMEM((tok, width), F32),
            pltpu.VMEM((STEP_DEVS, 2, width), F32),
            pltpu.VMEM((STEPS, width), F32),
            pltpu.VMEM((SEQ_DEVS, tok, 3 * HEAD_SIZE), BF16),
            pltpu.VMEM((SEQ_DEVS, STEPS, tok), F32),
            pltpu.VMEM((STEPS, 3 * HEAD_SIZE), F32),
            pltpu.VMEM((4, SEQ_DEVS, tok, 3 * HEAD_SIZE), BF16),
            pltpu.VMEM((2, STEP_DEVS, 4 * part, HEAD_SIZE), BF16),
            pltpu.VMEM((2, 4 * part, INNER), BF16),
            pltpu.VMEM((2, 4, part, width), F32),
            pltpu.VMEM((2, part, width), BF16),
            pltpu.VMEM((2, SEQ_DEVS, 16, lane4), BF16),
            pltpu.VMEM((2, SEQ_DEVS, 16, lane4), F32),
            pltpu.VMEM((2, part, width), F32),
            pltpu.VMEM((2, 16, lane4), F32),
            pltpu.VMEM((2, 4, part, width), BF16),
            pltpu.VMEM((8 * tok, width), BF16),
            pltpu.VMEM((8 * tok, 3 * INNER // 4), BF16),
            pltpu.VMEM((8 * tok, INNER // 4), BF16),
            pltpu.VMEM((2, tok, INNER), BF16),
            pltpu.VMEM((2, 2, half, width), F32),
            pltpu.VMEM((2, half, width), BF16),
            pltpu.VMEM((2, STEP_DEVS, 16, lane4), BF16),
            pltpu.VMEM((2, STEP_DEVS, 16, lane4), F32),
            pltpu.VMEM((2, half, width), F32),
            pltpu.VMEM((8 * half, 8 * tok), F32),
            pltpu.VMEM((8 * half, 8 * tok), F32),
            dma((3,)), dma((3,)), dma, dma((4,)),
            dma((15,)), dma((15,)), dma((3,)), dma((3,)), dma((4,)), dma((4,)), dma((7,)), dma((7,)),
            dma((2, 7)), dma((2,)),
            dma((3,)), dma((3,)), dma((2,)), dma((2,)), dma((3, 4)), dma((3, 4)), dma((8,)), dma((8,)),
            dma((2, 15)), dma((2, 15)), dma((2, 7)), dma((2, 7)), dma((2, 7)), dma((2, 7)),
            dma((2, 8)), dma((2, 8)), dma((2, 8)), dma((2, 8)),
            dma((2, 2, 7)), dma((2, 2, 7)), dma((2, 2)), dma((2, 15)), dma((2, 15)), dma((2, 15)), dma((2, 15)),
        ],
        compiler_params=pltpu.CompilerParams(
            collective_id=0, has_side_effects=True, vmem_limit_bytes=58 * 1024 * 1024),
        name="picard",
    )(te, start_state, qkv_weight, out_weight)
    return start_state[None] + (1.0 / STEPS) * sums


def solution(mesh):
    return jax.shard_map(
        on_device,
        mesh=mesh,
        in_specs=(P("seq", None), P("step"), P(), P("seq", None)),
        out_specs=P("step", "seq", None),
        check_vma=False,
    )
```
